256 devices in a mesh: ctx: 64 (over z, x, y_lo), head: 4 (over y_hi, core).
Axes of the slice: x: 4, y: 4 (y_hi: 2, y_lo: 2; y = y_hi * 2 + y_lo), z: 8, core: 2. Of those that a mesh axis runs over, the one named last changes fastest.
Arguments:
- queries: bfloat16 [16384, 4096], P('ctx', 'head'), may hold values from -12 to 12
- keys: bfloat16 [16384, 512], P('ctx', 'head'), may hold values from -4.5 to 4.5
- values: bfloat16 [16384, 512], P('ctx', 'head'), may hold values from -6 to 6
- out_weight: bfloat16 [4096, 8192], P('head', 'ctx'), may hold values from -0.09375 to 0.09375
- segment: int32 [16384], replicated, may hold values from 0 to 8, as said below
- placement: int32 [128], replicated, may hold values from 0 to 127, as said below
Outputs:
- projected: bfloat16 [16384, 8192], P('ctx', 'head')
The draws below stay inside these ranges and needn't reach their ends.
Inputs may be any that keep to these rules, and one draw needn't show every extreme that they name: `placement`: each stretch number appears in exactly one slot. `segment`: each image occupies consecutive positions, at most 1280, one image exactly 1280; each block of 2048 positions holds one image, and ids rise with position.
All inputs are finite; a program needn't handle non-finite values.
Results may differ from the reference program's by a relative error of at most 0.015.
Values may be sent and summed in bfloat16 or wider, within the bound.
No kernel may reach another device: no remote copies, remote signals or barrier semaphores. Data moves between devices by JAX's collectives and lax.ppermute only.
A program may use at most 64 MiB of HBM per device.

```python
import math
import jax
import jax.numpy as jnp
from jax import lax

D = 8192
QH = 32
KVH = 4
HD = 128
CH = 128
REGION = 2048
IMG_MAX = 1280
TOKENS = 16384
STRETCHES = 128
QDIM = 4096
N_HEAD = 4


def doc_layout(key):
    order_key = jax.random.fold_in(key, 101)
    order = jax.random.permutation(order_key, STRETCHES).astype(jnp.int32)
    regions = TOKENS // REGION
    length_key = jax.random.fold_in(key, 102)
    lengths = jax.random.randint(length_key, (regions,), IMG_MAX // 4, IMG_MAX + 1)
    pick_key = jax.random.fold_in(key, 103)
    biggest = jax.random.randint(pick_key, (), 0, regions)
    lengths = jnp.where(jnp.arange(regions) == biggest, IMG_MAX, lengths)
    start_key = jax.random.fold_in(key, 104)
    starts = jax.random.randint(start_key, (regions,), 0, REGION - IMG_MAX + 1)
    position = jnp.arange(TOKENS, dtype=jnp.int32)
    region = position // REGION
    offset = position % REGION
    inside = (offset >= starts[region]) & (offset < starts[region] + lengths[region])
    by_position = jnp.where(inside, region + 1, 0).astype(jnp.int32)
    stored_rows = jnp.arange(TOKENS, dtype=jnp.int32)
    stored = by_position[order[stored_rows // CH] * CH + stored_rows % CH]
    return (order, stored)


def draw_queries(key, part):
    key = jax.random.fold_in(key, 11)
    result = jax.random.truncated_normal(key, -4.0, 4.0, (TOKENS, QH * HD)) * 3.0
    return result.astype(jnp.bfloat16)


def draw_keys(key, part):
    key = jax.random.fold_in(key, 12)
    result = jax.random.truncated_normal(key, -4.0, 4.0, (TOKENS, KVH * HD))
    return result.astype(jnp.bfloat16)


def draw_segment(key, part):
    order, stored = doc_layout(key)
    return stored.astype(jnp.int32)


def draw_placement(key, part):
    order, stored = doc_layout(key)
    return order.astype(jnp.int32)


def level_of(rng, shape, shards, least, top_value):
    loudness = 1.0
    for dim, blocks in shards:
        draws = jax.random.uniform(jax.random.fold_in(jax.random.fold_in(rng, 6), dim), (blocks,), jnp.float32, least / len(shards), top_value / len(shards))
        loudness = loudness * jnp.repeat(jnp.exp(draws), shape[dim] // blocks).reshape((-1,) + (1,) * (len(shape) - 1 - dim))
    return loudness


def scatter_about(rng, extent, scale, bound, split=(), kind=jnp.bfloat16):
    factor_of = level_of(rng, extent, split, -0.22, 0.18) if split else 1.0
    values = jax.random.normal(rng, extent, jnp.float32) * scale * factor_of
    return jnp.minimum(jnp.maximum(values, -bound), bound).astype(kind)


def setup_inputs(seed: int = 0) -> dict:
    splits = jax.random.split(jax.random.key(seed), 7)
    return {
        "queries": draw_queries(jax.random.fold_in(splits[6], 71), 0),
        "keys": draw_keys(jax.random.fold_in(splits[6], 71), 0),
        "values": scatter_about(splits[2], (TOKENS, KVH * HD), 1.0, 6.0, ((0, 64), (1, 4))),
        "out_weight": scatter_about(splits[3], (QDIM, D), QDIM ** -0.5, 0.09375, ((0, 4), (1, 64))),
        "segment": draw_segment(jax.random.fold_in(splits[6], 71), 0),
        "placement": draw_placement(jax.random.fold_in(splits[6], 71), 0),
    }


def reference(queries, keys, values, out_weight, segment, placement):
    group = QH // KVH
    scale = 1.0 / math.sqrt(HD)
    index = jnp.arange(TOKENS, dtype=jnp.int32)
    position = placement[index // CH] * CH + index % CH
    block_rows = min(512, TOKENS)
    starts = jnp.arange(TOKENS // block_rows, dtype=jnp.int32) * block_rows
    head_outputs = []
    for kv_index in range(KVH):
        key_head = keys[:, kv_index * HD:(kv_index + 1) * HD].astype(jnp.float32)
        value_head = values[:, kv_index * HD:(kv_index + 1) * HD].astype(jnp.float32)
        query_head = queries[:, kv_index * group * HD:(kv_index + 1) * group * HD]

        def block_out(start):
            query_block = lax.dynamic_slice_in_dim(query_head, start, block_rows, 0)
            query_block = query_block.astype(jnp.float32).reshape(block_rows, group, HD)
            scores = jnp.einsum('qgd,kd->gqk', query_block, key_head) * scale
            query_pos = lax.dynamic_slice_in_dim(position, start, block_rows, 0)
            query_seg = lax.dynamic_slice_in_dim(segment, start, block_rows, 0)
            allowed = (position[None, :] <= query_pos[:, None]) | (segment[None, :] == query_seg[:, None]) & (query_seg[:, None] > 0)
            masked = jnp.where(allowed[None], scores, -jnp.inf)
            peak = lax.optimization_barrier(jnp.max(masked, axis=2, keepdims=True))
            weights = jnp.where(allowed[None], jnp.exp(masked - peak), 0.0)
            totals = lax.optimization_barrier(jnp.sum(weights, axis=2))
            rounded = lax.optimization_barrier(weights.astype(jnp.bfloat16)).astype(jnp.float32)
            mixed = jnp.einsum('gqk,kd->gqd', rounded, value_head) / totals[:, :, None]
            mixed = jnp.transpose(mixed, (1, 0, 2)).reshape(block_rows, group * HD)
            return mixed.astype(jnp.bfloat16)
        head_outputs.append(lax.map(block_out, starts).reshape(TOKENS, group * HD))
    attention = jnp.concatenate(head_outputs, axis=1)
    width_group = QDIM // N_HEAD
    summed = jnp.zeros((TOKENS, D), jnp.float32)
    for group_index in range(N_HEAD):
        partial_value = jnp.dot(attention[:, group_index * width_group:(group_index + 1) * width_group], out_weight[group_index * width_group:(group_index + 1) * width_group], preferred_element_type=jnp.float32)
        summed = summed + lax.optimization_barrier(partial_value.astype(jnp.bfloat16)).astype(jnp.float32)
    return summed.astype(jnp.bfloat16)
```

```python
import functools
import math

import jax
import jax.numpy as jnp
from jax import lax
from jax.experimental import pallas as pl
from jax.experimental.pallas import tpu as pltpu
from jax.sharding import Mesh
from jax.sharding import PartitionSpec as P

HD = 128
CH = 128
CPD = 2
Z, X, YL, YH, CORE = 8, 4, 2, 2, 2
NH = YH * CORE
ZX = Z * X
EVERY = ("z", "x", "ylo", "yhi", "core")
GROUP = 4
HEADS = 8
WIDE = HEADS * HD
LISTED = ZX * CPD
PART = 256
SCALE = 1.0 / math.sqrt(HD)
LEAST = 2.0**-80
MOST = 2.0**120
STAGES = ((0,), (1, 7), (2, 6), (3, 5), (4,))
STRETCHES_OF = [len(stage) * X * CPD for stage in STAGES]
STARTS = [sum(STRETCHES_OF[:i]) for i in range(len(STAGES))]
OWN_AND_FAR = YL * CPD
EMPTY = -1e30
SMEM = pl.BlockSpec(memory_space=pltpu.SMEM)
VMEM = pl.BlockSpec(memory_space=pltpu.VMEM)
NT = (((1,), (1,)), ((), ()))
ROWS = CPD * CH
SWAP = [(0, 1), (1, 0)]
VMEM_LIMIT = 24 << 20


def listed_rows(list_ref, which, entry):
    return pl.ds(pl.multiple_of(list_ref[which, entry] * CH, CH), CH)


def allowed_in(list_ref, seg_ref, entry, q_pos, q_seg):
    k_pos = list_ref[2, entry] * CH + lax.broadcasted_iota(jnp.int32, (CH, CH), 1)
    k_seg = seg_ref[pl.ds(list_ref[3, entry], 1), :]
    return (k_pos <= q_pos) | ((k_seg == q_seg) & (q_seg > 0))


def query_rows(info_ref, qseg_ref, i):
    q_pos = info_ref[0, i] * CH + lax.broadcasted_iota(jnp.int32, (CH, CH), 0)
    q_seg = jnp.broadcast_to(qseg_ref[i * CH : (i + 1) * CH, :], (CH, CH))
    return q_pos, q_seg


def load_queries(query_ref, q_refs, i):
    rows = slice(i % CPD * CH, (i % CPD + 1) * CH)
    for j in range(HEADS):
        query_ref[j * CH : (j + 1) * CH, :] = q_refs[i // CPD][rows, j * HD : (j + 1) * HD]


def load_pieces(kv_ref, pieces):
    row = 0
    for piece in pieces:
        rows = piece.shape[0]
        kv_ref[row : row + rows, :] = piece[...]
        row += rows


def plain_pass(i, stage, list_ref, info_ref, q_ref, kv_ref, qseg_ref, seg_ref, acc_ref):
    blocks = HEADS * CH // PART
    base = STARTS[stage]

    def group_step(g, masked):
        entries = [base + g * GROUP + e for e in range(GROUP)]
        key = jnp.concatenate([kv_ref[listed_rows(list_ref, 0, e), :] for e in entries], axis=0)
        value = jnp.concatenate([kv_ref[listed_rows(list_ref, 1, e), :] for e in entries], axis=0)
        value = jnp.concatenate([value, jnp.ones((GROUP * CH, HD), jnp.bfloat16)], axis=1)
        if masked:
            q_pos, q_seg = query_rows(info_ref, qseg_ref, i)
            allowed = jnp.concatenate(
                [allowed_in(list_ref, seg_ref, e, q_pos, q_seg) for e in entries], axis=1
            )
            allowed = jnp.concatenate([allowed] * (PART // CH), axis=0)

        def scores_of(block):
            query = q_ref[block * PART : (block + 1) * PART, :]
            return lax.dot_general(query, key, NT, preferred_element_type=jnp.float32)

        ahead = scores_of(0)
        for block in range(blocks):
            scores = ahead
            if block + 1 < blocks:
                ahead = scores_of(block + 1)
            weights = jnp.exp(scores * SCALE)
            if masked:
                weights = jnp.where(allowed, weights, 0.0)
            acc_ref[i, block * PART : (block + 1) * PART, :] += jnp.dot(
                weights.astype(jnp.bfloat16), value, preferred_element_type=jnp.float32
            )

    whole = info_ref[1 + stage, i] // GROUP
    end = (info_ref[1 + len(STAGES) + stage, i] + GROUP - 1) // GROUP
    lax.fori_loop(0, whole, lambda g, c: (group_step(g, False), c)[1], 0)
    lax.fori_loop(whole, end, lambda g, c: (group_step(g, True), c)[1], 0)


def safe_pass(
    i, list_ref, info_ref, q_ref, all_pieces, kv_ref, qseg_ref, seg_ref, out_ref, log_ref,
    top_ref, sum_ref, mix_ref,
):
    q_pos, q_seg = query_rows(info_ref, qseg_ref, i)
    top_ref[...] = jnp.full_like(top_ref, EMPTY)
    sum_ref[...] = jnp.zeros_like(sum_ref)
    mix_ref[...] = jnp.zeros_like(mix_ref)

    for stage, pieces in enumerate(all_pieces):
        load_pieces(kv_ref, pieces)

        def step(number, c, stage=stage):
            entry = STARTS[stage] + number
            allowed = allowed_in(list_ref, seg_ref, entry, q_pos, q_seg)
            allowed = jnp.concatenate([allowed] * HEADS, axis=0)
            scores = SCALE * lax.dot_general(
                q_ref[...], kv_ref[listed_rows(list_ref, 0, entry), :], NT,
                preferred_element_type=jnp.float32,
            )
            masked = jnp.where(allowed, scores, EMPTY)
            top = jnp.maximum(top_ref[...], jnp.max(masked, axis=1, keepdims=True))
            weights = jnp.where(allowed, jnp.exp(masked - top), 0.0)
            factor = jnp.exp(top_ref[...] - top)
            sum_ref[...] = sum_ref[...] * factor + jnp.sum(weights, axis=1, keepdims=True)
            mix_ref[...] = mix_ref[...] * factor + jnp.dot(
                weights.astype(jnp.bfloat16), kv_ref[listed_rows(list_ref, 1, entry), :],
                preferred_element_type=jnp.float32,
            )
            top_ref[...] = top
            return c

        lax.fori_loop(0, info_ref[1 + len(STAGES) + stage, i], step, 0)
    seen = sum_ref[...] > 0.0
    total = jnp.where(seen, sum_ref[...], 1.0)
    logs = jnp.where(seen, top_ref[...] + jnp.log(total), EMPTY)
    store_part(out_ref, log_ref, mix_ref[...] / total, logs)


def store_part(out_ref, log_ref, mixed, logs):
    for j in range(HEADS):
        rows = slice(j * CH, (j + 1) * CH)
        out_ref[:, j * HD : (j + 1) * HD] = mixed[rows].astype(out_ref.dtype)
        log_ref[j : j + 1, :] = logs[rows].T[0:1, :]


def attend_kernel(stage, *refs):
    list_ref, info_ref, q0_ref, q1_ref, qseg_ref, seg_ref = refs[:6]
    refs = refs[6:]
    if stage:
        acc_in_ref, refs = refs[0], refs[1:]
    last = stage == len(STAGES) - 1
    all_pieces = []
    for number in range(0 if last else stage, stage + 1):
        count = max(2, len(STAGES[number])) if number else 1
        all_pieces.append(refs[:count])
        refs = refs[count:]
    if last:
        outs, refs = refs[: 2 * OWN_AND_FAR], refs[2 * OWN_AND_FAR :]
        acc_ref, kv_ref, query_ref, top_ref, sum_ref, mix_ref = refs
    else:
        acc_ref, kv_ref, query_ref = refs
    load_pieces(kv_ref, all_pieces[-1])
    acc_ref[...] = acc_in_ref[...] if stage else jnp.zeros_like(acc_ref)
    for i in range(OWN_AND_FAR):
        load_queries(query_ref, (q0_ref, q1_ref), i)
        plain_pass(i, stage, list_ref, info_ref, query_ref, kv_ref, qseg_ref, seg_ref, acc_ref)
    if not last:
        return
    for i in range(OWN_AND_FAR):
        out_ref, log_ref = outs[2 * i], outs[2 * i + 1]
        fits = (jnp.min(acc_ref[i, :, HD:]) >= LEAST) & (jnp.max(acc_ref[i, :, HD:]) <= MOST)

        @pl.when(fits)
        def _(i=i, out_ref=out_ref, log_ref=log_ref):
            total = acc_ref[i, :, HD:]
            store_part(out_ref, log_ref, acc_ref[i, :, :HD] / total, jnp.log(total))

        @pl.when(jnp.logical_not(fits))
        def _(i=i, out_ref=out_ref, log_ref=log_ref):
            load_queries(query_ref, (q0_ref, q1_ref), i)
            safe_pass(
                i, list_ref, info_ref, query_ref, all_pieces, kv_ref, qseg_ref, seg_ref,
                out_ref, log_ref, top_ref, sum_ref, mix_ref,
            )


def attend(stage, listed, info, own_query, far_query, qseg, seg, acc, all_pieces):
    last = stage == len(STAGES) - 1
    pieces = [piece for part in (all_pieces if last else all_pieces[-1:]) for piece in part]
    state = pltpu.VMEM((HEADS * CH, HD), jnp.float32)
    total = (OWN_AND_FAR, HEADS * CH, 2 * HD)
    scratch = [
        pltpu.VMEM((2 * X * 2 * ROWS, HD), jnp.bfloat16),
        pltpu.VMEM((HEADS * CH, HD), jnp.bfloat16),
    ]
    if last:
        shapes = []
        for kind in (jnp.float32, jnp.bfloat16):
            for _ in range(CPD):
                shapes.append(jax.ShapeDtypeStruct((CH, WIDE), kind))
                shapes.append(jax.ShapeDtypeStruct((HEADS, CH), jnp.float32))
        scratch = [pltpu.VMEM(total, jnp.float32)] + scratch + [state] * 3
    else:
        shapes = [jax.ShapeDtypeStruct(total, jnp.float32)]
    begun = [acc] if stage else []
    work = STRETCHES_OF[stage] * CH * OWN_AND_FAR * HEADS * CH
    out = pl.pallas_call(
        functools.partial(attend_kernel, stage),
        out_shape=shapes,
        in_specs=[SMEM, SMEM] + [VMEM] * (4 + len(begun) + len(pieces)),
        out_specs=[VMEM] * len(shapes),
        scratch_shapes=scratch,
        input_output_aliases={6: 0} if stage and not last else {},
        compiler_params=pltpu.CompilerParams(vmem_limit_bytes=VMEM_LIMIT),
        cost_estimate=pl.CostEstimate(
            flops=12 * work * HD, bytes_accessed=4 << 20, transcendentals=work // 2
        ),
        name="attend",
    )(listed, info, own_query, far_query, qseg, seg, *begun, *pieces)
    return out if last else out[0]


def merge_kernel(own_ref, own_log_ref, got_ref, got_log_ref, out_ref):
    for j in range(HEADS):
        gap = got_log_ref[j : j + 1, :] - own_log_ref[j : j + 1, :]
        share = jnp.broadcast_to(1.0 / (1.0 + jnp.exp(gap)), (CH, CH)).T
        other = jnp.broadcast_to(1.0 / (1.0 + jnp.exp(-gap)), (CH, CH)).T
        cols = slice(j * HD, (j + 1) * HD)
        out_ref[:, cols] = (
            own_ref[:, cols] * share + got_ref[:, cols].astype(jnp.float32) * other
        ).astype(out_ref.dtype)


def merge(own, own_log, got, got_log):
    return pl.pallas_call(
        merge_kernel,
        out_shape=jax.ShapeDtypeStruct(got.shape, jnp.bfloat16),
        in_specs=[VMEM] * 4,
        out_specs=VMEM,
        name="merge",
    )(own, own_log, got, got_log)


def project_kernel(wide, index_ref, near0_ref, far0_ref, near1_ref, far1_ref, weight_ref, out_ref):
    lefts = []
    for h in range(NH):
        distance, other = index_ref[0, h], index_ref[1, h]
        both = [
            jnp.where(other == 0, near_ref[distance], far_ref[distance])
            for near_ref, far_ref in ((near0_ref, far0_ref), (near1_ref, far1_ref))
        ]
        lefts.append(jnp.concatenate(both, axis=0))
    for x in range(X):
        total = jnp.zeros((ROWS, 2 * CH), jnp.float32)
        for h in range(NH):
            right = jnp.concatenate([weight_ref[h, e, x] for e in range(2)], axis=1)
            total += jnp.dot(lefts[h], right, preferred_element_type=jnp.float32)
        start = x * 2 * CH
        if wide:
            start = pl.multiple_of(index_ref[2, 0] * (X * 2 * CH) + start, 2 * CH)
        out_ref[:, pl.ds(start, 2 * CH)] = total.astype(out_ref.dtype)


def project(index, gathered, weight, wide):
    feats = weight.shape[3]
    columns = X * 2 * CH
    return pl.pallas_call(
        functools.partial(project_kernel, wide),
        out_shape=jax.ShapeDtypeStruct((ROWS, YL * columns if wide else columns), jnp.bfloat16),
        in_specs=[SMEM] + [VMEM] * 5,
        out_specs=VMEM,
        compiler_params=pltpu.CompilerParams(vmem_limit_bytes=VMEM_LIMIT),
        cost_estimate=pl.CostEstimate(
            flops=2 * ROWS * NH * feats * columns, bytes_accessed=12 << 20, transcendentals=0
        ),
        name="project",
    )(index, *gathered, weight)


def device_number(z, x, yl, h):
    return ((z * X + x) * YL + yl) * NH + h


def weight_moves():
    moves = []
    for z in range(Z):
        for x in range(X):
            for yl in range(YL):
                for h in range(NH):
                    to = device_number(2 * h + yl, x, z % 2, z // 2)
                    moves.append((device_number(z, x, yl, h), to))
    return moves


def fetch(array, axis, by):
    if axis == "y":
        spots = [y % YL * YH + y // YL for y in range(YH * YL)]
        axis = ("ylo", "yhi")
    else:
        spots = list(range({"z": Z, "x": X}[axis]))
    count = len(spots)
    return lax.ppermute(array, axis, [(spots[i], spots[(i - by) % count]) for i in range(count)])


def around(block, axis, count):
    ups, downs = [block], [block]
    for _ in range(count // 2 - 1):
        ups.append(fetch(ups[-1], axis, 1))
        downs.append(fetch(downs[-1], axis, -1))
    half = block.shape[0] // 2
    far = [fetch(ups[-1][:half], axis, 1), fetch(downs[-1][half:], axis, -1)]
    return ups + far + downs[:0:-1]


def gather_x(keys, values):
    block = jnp.concatenate([keys, values], axis=0)
    return [block] + [fetch(block, "x", by) for by in (1, 2, -1)]


def gather_z(blocks):
    rows = around(jnp.concatenate(blocks, axis=0), "z", Z)
    return [(rows[0],)] + [(rows[i], rows[-i]) for i in range(1, Z // 2)] + [tuple(rows[4:6])]


def list_stretches(placement, z, x, ylo):
    item = jnp.arange(LISTED, dtype=jnp.int32)
    per = X * CPD
    order = [dz for stage in STAGES for dz in stage]
    dz = jnp.asarray([order[i // per] for i in range(LISTED)], jnp.int32)
    dx, t = item // CPD % X, item % CPD
    stage = jnp.asarray([n for n, count in enumerate(STRETCHES_OF) for _ in range(count)], jnp.int32)
    start = jnp.asarray([STARTS[n] for n, count in enumerate(STRETCHES_OF) for _ in range(count)], jnp.int32)
    slot = (((z + dz) % Z * X + (x + dx) % X) * YL + ylo) * CPD + t
    pos = placement[slot]
    row = (item - start) // CPD * (2 * CPD) + t
    facts = jnp.stack([row, row + CPD, pos, slot])
    together = stage[None, :] == stage[:, None]
    rank = start + jnp.sum((together & (pos[None, :] < pos[:, None])).astype(jnp.int32), axis=1)
    hit = rank[None, :] == item[:, None]
    return pos, stage, jnp.sum(jnp.where(hit[None], facts[:, None, :], 0), axis=2)


def body(queries, keys, values, out_weight, segment, placement):
    z, x, ylo = lax.axis_index("z"), lax.axis_index("x"), lax.axis_index("ylo")
    yhi, core = lax.axis_index("yhi"), lax.axis_index("core")
    device = (z * X + x) * YL + ylo
    feats = queries.shape[1]

    blocks = gather_x(keys, values)
    far_queries = lax.ppermute(queries, "ylo", SWAP)

    labels = segment.reshape(-1, CH)
    pair_devices = jnp.stack([device, device + 1 - 2 * ylo])
    pair_slots = pair_devices[:, None] * CPD + jnp.arange(CPD, dtype=jnp.int32)[None, :]
    pair_slots = pair_slots.reshape(OWN_AND_FAR)
    pos = placement[pair_slots]
    pair_labels = labels[pair_slots]
    last = pair_labels[:, CH - 1, None]
    beyond = (placement > pos[:, None]) & (labels[:, 0] == last) & (last > 0)
    last_pos = pos + jnp.sum(beyond.astype(jnp.int32), axis=1)
    list_pos, list_stage, listed = list_stretches(placement, z, x, ylo)
    in_stage = list_stage == jnp.arange(len(STAGES), dtype=jnp.int32)[:, None, None]
    full = jnp.sum((in_stage & (list_pos < pos[:, None])).astype(jnp.int32), axis=2)
    some = jnp.sum((in_stage & (list_pos <= last_pos[:, None])).astype(jnp.int32), axis=2)
    info = jnp.concatenate([pos[None], full, some], axis=0)
    qseg = pair_labels.reshape(OWN_AND_FAR * CH, 1)

    moved_weight = lax.ppermute(out_weight, EVERY, weight_moves())
    blocks, listed, info, qseg, moved_weight, far_queries = lax.optimization_barrier(
        (blocks, listed, info, qseg, moved_weight, far_queries)
    )
    weight = lax.all_gather(moved_weight, ("z", "x"), axis=0, tiled=True)
    weight = weight.reshape(NH, 2, X, feats, CH)
    stages = gather_z(blocks)
    state = None
    for stage in range(len(STAGES)):
        state = attend(
            stage, listed, info, queries, far_queries, qseg, labels, state, stages[: stage + 1]
        )
    parts = []
    for t in range(CPD):
        own, own_log, far, far_log = state[2 * t : 2 * t + 2] + state[2 * (CPD + t) : 2 * (CPD + t) + 2]
        parts.append((own, own_log, lax.ppermute(far, "ylo", SWAP), lax.ppermute(far_log, "ylo", SWAP)))
    gathered = []
    for t, part in enumerate(parts):
        near = jnp.concatenate(around(merge(*part), "y", YH * YL), axis=0)
        near = near.reshape(YH * YL, CH, feats)
        if t == CPD - 1:
            near, weight = lax.optimization_barrier((near, weight))
        gathered += [near, lax.ppermute(near, "core", SWAP)]

    def project_group(group, wide):
        h = jnp.arange(NH, dtype=jnp.int32)
        y = h // CORE * YL + group
        distance = (y - (yhi * YL + ylo) + YH * YL) % (YH * YL)
        index = jnp.stack([distance, (h % CORE) ^ core, jnp.broadcast_to(ylo, h.shape)])
        return project(index, gathered, weight, wide)

    theirs = project_group(1 - ylo, False)
    received = lax.ppermute(theirs, "ylo", SWAP)
    mine = project_group(ylo, True)
    return lax.dynamic_update_slice(mine, received, (0, (1 - ylo) * received.shape[1]))


def solution(mesh):
    parts = Mesh(mesh.devices.reshape(Z, X, YL, YH, CORE), EVERY)
    ctx, head = ("z", "x", "ylo"), ("yhi", "core")
    in_specs = (P(ctx, head), P(ctx, head), P(ctx, head), P(head, ctx), P(), P())
    return jax.shard_map(
        body, mesh=parts, in_specs=in_specs, out_specs=P(ctx, head), check_vma=False
    )
```

```python
import functools
import math

import jax
import jax.numpy as jnp
from jax import lax
from jax.experimental import pallas as pl
from jax.experimental.pallas import tpu as pltpu
from jax.sharding import Mesh
from jax.sharding import PartitionSpec as P

HD = 128
CH = 128
CPD = 2
Z, X, YL, YH, CORE = 8, 4, 2, 2, 2
NH = YH * CORE
ZX = Z * X
EVERY = ("z", "x", "ylo", "yhi", "core")
GROUP = 4
HEADS = 8
WIDE = HEADS * HD
LISTED = ZX * CPD
PART = 256
SCALE = 1.0 / math.sqrt(HD)
LEAST = 2.0**-80
MOST = 2.0**100
STAGES = ((0,), (1, 7), (2, 6), (3, 5), (4,))
STRETCHES_OF = [len(stage) * X * CPD for stage in STAGES]
STARTS = [sum(STRETCHES_OF[:i]) for i in range(len(STAGES))]
OWN_AND_FAR = YL * CPD
EMPTY = -1e30
SMEM = pl.BlockSpec(memory_space=pltpu.SMEM)
VMEM = pl.BlockSpec(memory_space=pltpu.VMEM)
NT = (((1,), (1,)), ((), ()))
ROWS = CPD * CH
SWAP = [(0, 1), (1, 0)]
VMEM_LIMIT = 24 << 20


def listed_rows(list_ref, which, entry):
    return pl.ds(pl.multiple_of(list_ref[which, entry] * CH, CH), CH)


def allowed_in(list_ref, seg_ref, entry, q_pos, q_seg):
    k_pos = list_ref[2, entry] * CH + lax.broadcasted_iota(jnp.int32, (CH, CH), 1)
    k_seg = seg_ref[pl.ds(list_ref[3, entry], 1), :]
    return (k_pos <= q_pos) | ((k_seg == q_seg) & (q_seg > 0))


def query_rows(info_ref, qseg_ref, i):
    q_pos = info_ref[0, i] * CH + lax.broadcasted_iota(jnp.int32, (CH, CH), 0)
    q_seg = jnp.broadcast_to(qseg_ref[i * CH : (i + 1) * CH, :], (CH, CH))
    return q_pos, q_seg


def load_queries(query_ref, q_refs, i):
    rows = slice(i % CPD * CH, (i % CPD + 1) * CH)
    for j in range(HEADS):
        query_ref[j * CH : (j + 1) * CH, :] = q_refs[i // CPD][rows, j * HD : (j + 1) * HD]


def load_pieces(kv_ref, pieces):
    row = 0
    for piece in pieces:
        rows = piece.shape[0]
        kv_ref[row : row + rows, :] = piece[...]
        row += rows


def plain_pass(i, stage, list_ref, info_ref, q_ref, kv_ref, qseg_ref, seg_ref, acc_ref):
    blocks = HEADS * CH // PART
    base = STARTS[stage]

    def group_step(g, masked):
        entries = [base + g * GROUP + e for e in range(GROUP)]
        key = jnp.concatenate([kv_ref[listed_rows(list_ref, 0, e), :] for e in entries], axis=0)
        value = jnp.concatenate([kv_ref[listed_rows(list_ref, 1, e), :] for e in entries], axis=0)
        value = jnp.concatenate([value, jnp.ones((GROUP * CH, HD), jnp.bfloat16)], axis=1)
        if masked:
            q_pos, q_seg = query_rows(info_ref, qseg_ref, i)
            allowed = jnp.concatenate(
                [allowed_in(list_ref, seg_ref, e, q_pos, q_seg) for e in entries], axis=1
            )
            allowed = jnp.concatenate([allowed] * (PART // CH), axis=0)

        def scores_of(block):
            query = q_ref[block * PART : (block + 1) * PART, :]
            return lax.dot_general(query, key, NT, preferred_element_type=jnp.float32)

        ahead = scores_of(0)
        for block in range(blocks):
            scores = ahead
            if block + 1 < blocks:
                ahead = scores_of(block + 1)
            weights = jnp.exp(scores * SCALE)
            if masked:
                weights = jnp.where(allowed, weights, 0.0)
            acc_ref[i, block * PART : (block + 1) * PART, :] += jnp.dot(
                weights.astype(jnp.bfloat16), value, preferred_element_type=jnp.float32
            )

    whole = info_ref[1 + stage, i] // GROUP
    end = (info_ref[1 + len(STAGES) + stage, i] + GROUP - 1) // GROUP
    lax.fori_loop(0, whole, lambda g, c: (group_step(g, False), c)[1], 0)
    lax.fori_loop(whole, end, lambda g, c: (group_step(g, True), c)[1], 0)


def safe_pass(
    i, list_ref, info_ref, q_ref, all_pieces, kv_ref, qseg_ref, seg_ref, out_ref, stat_ref,
    top_ref, sum_ref, mix_ref,
):
    q_pos, q_seg = query_rows(info_ref, qseg_ref, i)
    top_ref[...] = jnp.full_like(top_ref, EMPTY)
    sum_ref[...] = jnp.zeros_like(sum_ref)
    mix_ref[...] = jnp.zeros_like(mix_ref)

    for stage, pieces in enumerate(all_pieces):
        load_pieces(kv_ref, pieces)

        def step(number, c, stage=stage):
            entry = STARTS[stage] + number
            allowed = allowed_in(list_ref, seg_ref, entry, q_pos, q_seg)
            allowed = jnp.concatenate([allowed] * HEADS, axis=0)
            scores = SCALE * lax.dot_general(
                q_ref[...], kv_ref[listed_rows(list_ref, 0, entry), :], NT,
                preferred_element_type=jnp.float32,
            )
            masked = jnp.where(allowed, scores, EMPTY)
            top = jnp.maximum(top_ref[...], jnp.max(masked, axis=1, keepdims=True))
            weights = jnp.where(allowed, jnp.exp(masked - top), 0.0)
            factor = jnp.exp(top_ref[...] - top)
            sum_ref[...] = sum_ref[...] * factor + jnp.sum(weights, axis=1, keepdims=True)
            mix_ref[...] = mix_ref[...] * factor + jnp.dot(
                weights.astype(jnp.bfloat16), kv_ref[listed_rows(list_ref, 1, entry), :],
                preferred_element_type=jnp.float32,
            )
            top_ref[...] = top
            return c

        lax.fori_loop(0, info_ref[1 + len(STAGES) + stage, i], step, 0)
    store_mixed(out_ref, mix_ref[...])
    store_stat(stat_ref, 0, sum_ref)
    store_stat(stat_ref, HEADS, top_ref)
    seen = stat_ref[:HEADS, :] > 0.0
    total = jnp.where(seen, stat_ref[:HEADS, :], 1.0)
    stat_ref[HEADS:, :] = jnp.where(seen, stat_ref[HEADS:, :] + jnp.log(total), EMPTY)
    stat_ref[:HEADS, :] = total


def store_mixed(out_ref, mixed):
    for j in range(HEADS):
        out_ref[:, j * HD : (j + 1) * HD] = mixed[j * CH : (j + 1) * CH].astype(out_ref.dtype)


def store_stat(stat_ref, start, rows_ref):
    for j in range(HEADS):
        stat_ref[start + j : start + j + 1, :] = rows_ref[j * CH : (j + 1) * CH, :].T[0:1, :]


def attend_kernel(stage, *refs):
    list_ref, info_ref, q0_ref, q1_ref, qseg_ref, seg_ref = refs[:6]
    refs = refs[6:]
    if stage:
        acc_in_ref, refs = refs[0], refs[1:]
    last = stage == len(STAGES) - 1
    all_pieces = []
    for number in range(0 if last else stage, stage + 1):
        count = max(2, len(STAGES[number])) if number else 1
        all_pieces.append(refs[:count])
        refs = refs[count:]
    if last:
        outs, refs = refs[: 2 * OWN_AND_FAR], refs[2 * OWN_AND_FAR :]
        acc_ref, kv_ref, query_ref, top_ref, sum_ref, mix_ref = refs
    else:
        acc_ref, kv_ref, query_ref = refs
    load_pieces(kv_ref, all_pieces[-1])
    acc_ref[...] = acc_in_ref[...] if stage else jnp.zeros_like(acc_ref)
    for i in range(OWN_AND_FAR):
        load_queries(query_ref, (q0_ref, q1_ref), i)
        plain_pass(i, stage, list_ref, info_ref, query_ref, kv_ref, qseg_ref, seg_ref, acc_ref)
    if not last:
        return
    for i in range(OWN_AND_FAR):
        out_ref, stat_ref = outs[2 * i], outs[2 * i + 1]
        store_stat(stat_ref, 0, acc_ref.at[i, :, HD:])
        total = stat_ref[:HEADS, :]
        fits = (jnp.min(total) >= LEAST) & (jnp.max(total) <= MOST)
        stat_ref[HEADS:, :] = jnp.log(total)
        store_mixed(out_ref, acc_ref[i, :, :HD])

        @pl.when(jnp.logical_not(fits))
        def _(i=i, out_ref=out_ref, stat_ref=stat_ref):
            load_queries(query_ref, (q0_ref, q1_ref), i)
            safe_pass(
                i, list_ref, info_ref, query_ref, all_pieces, kv_ref, qseg_ref, seg_ref,
                out_ref, stat_ref, top_ref, sum_ref, mix_ref,
            )


def attend(stage, listed, info, own_query, far_query, qseg, seg, acc, all_pieces):
    last = stage == len(STAGES) - 1
    pieces = [piece for part in (all_pieces if last else all_pieces[-1:]) for piece in part]
    state = pltpu.VMEM((HEADS * CH, HD), jnp.float32)
    total = (OWN_AND_FAR, HEADS * CH, 2 * HD)
    scratch = [
        pltpu.VMEM((2 * X * 2 * ROWS, HD), jnp.bfloat16),
        pltpu.VMEM((HEADS * CH, HD), jnp.bfloat16),
    ]
    if last:
        shapes = []
        for kind in (jnp.float32, jnp.bfloat16):
            for _ in range(CPD):
                shapes.append(jax.ShapeDtypeStruct((CH, WIDE), kind))
                shapes.append(jax.ShapeDtypeStruct((2 * HEADS, CH), jnp.float32))
        scratch = [pltpu.VMEM(total, jnp.float32)] + scratch + [state] * 3
    else:
        shapes = [jax.ShapeDtypeStruct(total, jnp.float32)]
    begun = [acc] if stage else []
    work = STRETCHES_OF[stage] * CH * OWN_AND_FAR * HEADS * CH
    out = pl.pallas_call(
        functools.partial(attend_kernel, stage),
        out_shape=shapes,
        in_specs=[SMEM, SMEM] + [VMEM] * (4 + len(begun) + len(pieces)),
        out_specs=[VMEM] * len(shapes),
        scratch_shapes=scratch,
        input_output_aliases={6: 0} if stage and not last else {},
        compiler_params=pltpu.CompilerParams(vmem_limit_bytes=VMEM_LIMIT),
        cost_estimate=pl.CostEstimate(
            flops=12 * work * HD, bytes_accessed=4 << 20, transcendentals=work // 2
        ),
        name="attend",
    )(listed, info, own_query, far_query, qseg, seg, *begun, *pieces)
    return out if last else out[0]


def merge_kernel(own_ref, own_stat_ref, got_ref, got_stat_ref, out_ref):
    gap = got_stat_ref[HEADS:, :] - own_stat_ref[HEADS:, :]
    own_share = 1.0 / ((1.0 + jnp.exp(gap)) * own_stat_ref[:HEADS, :])
    got_share = 1.0 / ((1.0 + jnp.exp(-gap)) * got_stat_ref[:HEADS, :])
    for j in range(HEADS):
        own = jnp.broadcast_to(own_share[j : j + 1, :], (CH, CH)).T
        got = jnp.broadcast_to(got_share[j : j + 1, :], (CH, CH)).T
        cols = slice(j * HD, (j + 1) * HD)
        out_ref[:, cols] = (
            own_ref[:, cols] * own + got_ref[:, cols].astype(jnp.float32) * got
        ).astype(out_ref.dtype)


def merge(own, own_stat, got, got_stat):
    return pl.pallas_call(
        merge_kernel,
        out_shape=jax.ShapeDtypeStruct(got.shape, jnp.bfloat16),
        in_specs=[VMEM] * 4,
        out_specs=VMEM,
        name="merge",
    )(own, own_stat, got, got_stat)


def project_kernel(wide, index_ref, near0_ref, far0_ref, near1_ref, far1_ref, weight_ref, out_ref):
    lefts = []
    for h in range(NH):
        distance, other = index_ref[0, h], index_ref[1, h]
        both = [
            jnp.where(other == 0, near_ref[distance], far_ref[distance])
            for near_ref, far_ref in ((near0_ref, far0_ref), (near1_ref, far1_ref))
        ]
        lefts.append(jnp.concatenate(both, axis=0))
    for x in range(X):
        total = jnp.zeros((ROWS, 2 * CH), jnp.float32)
        for h in range(NH):
            right = jnp.concatenate([weight_ref[h, e, x] for e in range(2)], axis=1)
            total += jnp.dot(lefts[h], right, preferred_element_type=jnp.float32)
        start = x * 2 * CH
        if wide:
            start = pl.multiple_of(index_ref[2, 0] * (X * 2 * CH) + start, 2 * CH)
        out_ref[:, pl.ds(start, 2 * CH)] = total.astype(out_ref.dtype)


def project(index, gathered, weight, wide):
    feats = weight.shape[3]
    columns = X * 2 * CH
    return pl.pallas_call(
        functools.partial(project_kernel, wide),
        out_shape=jax.ShapeDtypeStruct((ROWS, YL * columns if wide else columns), jnp.bfloat16),
        in_specs=[SMEM] + [VMEM] * 5,
        out_specs=VMEM,
        compiler_params=pltpu.CompilerParams(vmem_limit_bytes=VMEM_LIMIT),
        cost_estimate=pl.CostEstimate(
            flops=2 * ROWS * NH * feats * columns, bytes_accessed=12 << 20, transcendentals=0
        ),
        name="project",
    )(index, *gathered, weight)


def device_number(z, x, yl, h):
    return ((z * X + x) * YL + yl) * NH + h


def weight_moves():
    moves = []
    for z in range(Z):
        for x in range(X):
            for yl in range(YL):
                for h in range(NH):
                    to = device_number(2 * h + yl, x, z % 2, z // 2)
                    moves.append((device_number(z, x, yl, h), to))
    return moves


def fetch(array, axis, by):
    if axis == "y":
        spots = [y % YL * YH + y // YL for y in range(YH * YL)]
        axis = ("ylo", "yhi")
    else:
        spots = list(range({"z": Z, "x": X}[axis]))
    count = len(spots)
    return lax.ppermute(array, axis, [(spots[i], spots[(i - by) % count]) for i in range(count)])


def around(block, axis, count):
    ups, downs = [block], [block]
    for _ in range(count // 2 - 1):
        ups.append(fetch(ups[-1], axis, 1))
        downs.append(fetch(downs[-1], axis, -1))
    half = block.shape[0] // 2
    far = [fetch(ups[-1][:half], axis, 1), fetch(downs[-1][half:], axis, -1)]
    return ups + far + downs[:0:-1]


def gather_x(keys, values):
    block = jnp.concatenate([keys, values], axis=0)
    return [block] + [fetch(block, "x", by) for by in (1, 2, -1)]


def gather_z(blocks):
    rows = around(jnp.concatenate(blocks, axis=0), "z", Z)
    return [(rows[0],)] + [(rows[i], rows[-i]) for i in range(1, Z // 2)] + [tuple(rows[4:6])]


def list_stretches(placement, z, x, ylo):
    item = jnp.arange(LISTED, dtype=jnp.int32)
    per = X * CPD
    order = [dz for stage in STAGES for dz in stage]
    dz = jnp.asarray([order[i // per] for i in range(LISTED)], jnp.int32)
    dx, t = item // CPD % X, item % CPD
    stage = jnp.asarray([n for n, count in enumerate(STRETCHES_OF) for _ in range(count)], jnp.int32)
    start = jnp.asarray([STARTS[n] for n, count in enumerate(STRETCHES_OF) for _ in range(count)], jnp.int32)
    slot = (((z + dz) % Z * X + (x + dx) % X) * YL + ylo) * CPD + t
    pos = placement[slot]
    row = (item - start) // CPD * (2 * CPD) + t
    facts = jnp.stack([row, row + CPD, pos, slot])
    together = stage[None, :] == stage[:, None]
    rank = start + jnp.sum((together & (pos[None, :] < pos[:, None])).astype(jnp.int32), axis=1)
    hit = rank[None, :] == item[:, None]
    return pos, stage, jnp.sum(jnp.where(hit[None], facts[:, None, :], 0), axis=2)


def body(queries, keys, values, out_weight, segment, placement):
    z, x, ylo = lax.axis_index("z"), lax.axis_index("x"), lax.axis_index("ylo")
    yhi, core = lax.axis_index("yhi"), lax.axis_index("core")
    device = (z * X + x) * YL + ylo
    feats = queries.shape[1]

    blocks = gather_x(keys, values)
    far_queries = lax.ppermute(queries, "ylo", SWAP)

    labels = segment.reshape(-1, CH)
    pair_devices = jnp.stack([device, device + 1 - 2 * ylo])
    pair_slots = pair_devices[:, None] * CPD + jnp.arange(CPD, dtype=jnp.int32)[None, :]
    pair_slots = pair_slots.reshape(OWN_AND_FAR)
    pos = placement[pair_slots]
    pair_labels = labels[pair_slots]
    last = pair_labels[:, CH - 1, None]
    beyond = (placement > pos[:, None]) & (labels[:, 0] == last) & (last > 0)
    last_pos = pos + jnp.sum(beyond.astype(jnp.int32), axis=1)
    list_pos, list_stage, listed = list_stretches(placement, z, x, ylo)
    in_stage = list_stage == jnp.arange(len(STAGES), dtype=jnp.int32)[:, None, None]
    full = jnp.sum((in_stage & (list_pos < pos[:, None])).astype(jnp.int32), axis=2)
    some = jnp.sum((in_stage & (list_pos <= last_pos[:, None])).astype(jnp.int32), axis=2)
    info = jnp.concatenate([pos[None], full, some], axis=0)
    qseg = pair_labels.reshape(OWN_AND_FAR * CH, 1)

    moved_weight = lax.ppermute(out_weight, EVERY, weight_moves())
    blocks, listed, info, qseg = lax.optimization_barrier((blocks, listed, info, qseg))
    weight = lax.all_gather(moved_weight, ("z", "x"), axis=0, tiled=True)
    weight = weight.reshape(NH, 2, X, feats, CH)
    stages = gather_z(blocks)
    state = None
    for stage in range(len(STAGES)):
        state = attend(
            stage, listed, info, queries, far_queries, qseg, labels, state, stages[: stage + 1]
        )
    parts = []
    for t in range(CPD):
        own, own_log, far, far_log = state[2 * t : 2 * t + 2] + state[2 * (CPD + t) : 2 * (CPD + t) + 2]
        parts.append((own, own_log, lax.ppermute(far, "ylo", SWAP), lax.ppermute(far_log, "ylo", SWAP)))
    gathered = []
    for t, part in enumerate(parts):
        merged = merge(*part)
        up, down = fetch(merged, "y", 1), fetch(merged, "y", -1)
        if t == CPD - 1:
            up, weight = lax.optimization_barrier((up, weight))
        far = [fetch(up[: CH // 2], "y", 1), fetch(down[CH // 2 :], "y", -1)]
        near = jnp.concatenate([merged, up] + far + [down], axis=0).reshape(YH * YL, CH, feats)
        gathered += [near, lax.ppermute(near, "core", SWAP)]

    def project_group(group, wide):
        h = jnp.arange(NH, dtype=jnp.int32)
        y = h // CORE * YL + group
        distance = (y - (yhi * YL + ylo) + YH * YL) % (YH * YL)
        index = jnp.stack([distance, (h % CORE) ^ core, jnp.broadcast_to(ylo, h.shape)])
        return project(index, gathered, weight, wide)

    theirs = project_group(1 - ylo, False)
    received = lax.ppermute(theirs, "ylo", SWAP)
    mine = project_group(ylo, True)
    return lax.dynamic_update_slice(mine, received, (0, (1 - ylo) * received.shape[1]))


def solution(mesh):
    parts = Mesh(mesh.devices.reshape(Z, X, YL, YH, CORE), EVERY)
    ctx, head = ("z", "x", "ylo"), ("yhi", "core")
    in_specs = (P(ctx, head), P(ctx, head), P(ctx, head), P(head, ctx), P(), P())
    return jax.shard_map(
        body, mesh=parts, in_specs=in_specs, out_specs=P(ctx, head), check_vma=False
    )
```

```python
import functools
import math

import jax
import jax.numpy as jnp
from jax import lax
from jax.experimental import pallas as pl
from jax.experimental.pallas import tpu as pltpu
from jax.sharding import Mesh
from jax.sharding import PartitionSpec as P

HD = 128
CH = 128
CPD = 2
Z, X, YL, YH, CORE = 8, 4, 2, 2, 2
NH = YH * CORE
ZX = Z * X
EVERY = ("z", "x", "ylo", "yhi", "core")
GROUP = 4
HEADS = 8
WIDE = HEADS * HD
LISTED = ZX * CPD
PART = 256
SCALE = 1.0 / math.sqrt(HD)
LEAST = 2.0**-80
MOST = 2.0**100
STAGES = ((0,), (1, 7), (2, 6), (3, 5), (4,))
STRETCHES_OF = [len(stage) * X * CPD for stage in STAGES]
STARTS = [sum(STRETCHES_OF[:i]) for i in range(len(STAGES))]
OWN_AND_FAR = YL * CPD
EMPTY = -1e30
SMEM = pl.BlockSpec(memory_space=pltpu.SMEM)
VMEM = pl.BlockSpec(memory_space=pltpu.VMEM)
NT = (((1,), (1,)), ((), ()))
ROWS = CPD * CH
SWAP = [(0, 1), (1, 0)]
VMEM_LIMIT = 24 << 20


def listed_rows(list_ref, which, entry):
    return pl.ds(pl.multiple_of(list_ref[which, entry] * CH, CH), CH)


def allowed_in(list_ref, seg_ref, entry, q_pos, q_seg):
    k_pos = list_ref[2, entry] * CH + lax.broadcasted_iota(jnp.int32, (CH, CH), 1)
    k_seg = seg_ref[pl.ds(list_ref[3, entry], 1), :]
    return (k_pos <= q_pos) | ((k_seg == q_seg) & (q_seg > 0))


def query_rows(info_ref, qseg_ref, i):
    q_pos = info_ref[0, i] * CH + lax.broadcasted_iota(jnp.int32, (CH, CH), 0)
    q_seg = jnp.broadcast_to(qseg_ref[i * CH : (i + 1) * CH, :], (CH, CH))
    return q_pos, q_seg


def load_queries(query_ref, q_refs, i):
    rows = slice(i % CPD * CH, (i % CPD + 1) * CH)
    for j in range(HEADS):
        query_ref[j * CH : (j + 1) * CH, :] = q_refs[i // CPD][rows, j * HD : (j + 1) * HD]


def load_pieces(kv_ref, pieces):
    row = 0
    for piece in pieces:
        rows = piece.shape[0]
        kv_ref[row : row + rows, :] = piece[...]
        row += rows


def plain_pass(i, stage, list_ref, info_ref, q_ref, kv_ref, qseg_ref, seg_ref, acc_ref):
    blocks = HEADS * CH // PART
    base = STARTS[stage]

    def group_step(g, masked):
        entries = [base + g * GROUP + e for e in range(GROUP)]
        key = jnp.concatenate([kv_ref[listed_rows(list_ref, 0, e), :] for e in entries], axis=0)
        value = jnp.concatenate([kv_ref[listed_rows(list_ref, 1, e), :] for e in entries], axis=0)
        value = jnp.concatenate([value, jnp.ones((GROUP * CH, HD), jnp.bfloat16)], axis=1)
        if masked:
            q_pos, q_seg = query_rows(info_ref, qseg_ref, i)
            allowed = jnp.concatenate(
                [allowed_in(list_ref, seg_ref, e, q_pos, q_seg) for e in entries], axis=1
            )
            allowed = jnp.concatenate([allowed] * (PART // CH), axis=0)

        def scores_of(block):
            query = q_ref[block * PART : (block + 1) * PART, :]
            return lax.dot_general(query, key, NT, preferred_element_type=jnp.float32)

        ahead = scores_of(0)
        for block in range(blocks):
            scores = ahead
            if block + 1 < blocks:
                ahead = scores_of(block + 1)
            weights = jnp.exp(scores * SCALE)
            if masked:
                weights = jnp.where(allowed, weights, 0.0)
            acc_ref[i, block * PART : (block + 1) * PART, :] += jnp.dot(
                weights.astype(jnp.bfloat16), value, preferred_element_type=jnp.float32
            )

    whole = info_ref[1 + stage, i] // GROUP
    end = (info_ref[1 + len(STAGES) + stage, i] + GROUP - 1) // GROUP
    lax.fori_loop(0, whole, lambda g, c: (group_step(g, False), c)[1], 0)
    lax.fori_loop(whole, end, lambda g, c: (group_step(g, True), c)[1], 0)


def safe_pass(
    i, list_ref, info_ref, q_ref, all_pieces, kv_ref, qseg_ref, seg_ref, out_ref, stat_ref,
    top_ref, sum_ref, mix_ref,
):
    q_pos, q_seg = query_rows(info_ref, qseg_ref, i)
    top_ref[...] = jnp.full_like(top_ref, EMPTY)
    sum_ref[...] = jnp.zeros_like(sum_ref)
    mix_ref[...] = jnp.zeros_like(mix_ref)

    for stage, pieces in enumerate(all_pieces):
        load_pieces(kv_ref, pieces)

        def step(number, c, stage=stage):
            entry = STARTS[stage] + number
            allowed = allowed_in(list_ref, seg_ref, entry, q_pos, q_seg)
            allowed = jnp.concatenate([allowed] * HEADS, axis=0)
            scores = SCALE * lax.dot_general(
                q_ref[...], kv_ref[listed_rows(list_ref, 0, entry), :], NT,
                preferred_element_type=jnp.float32,
            )
            masked = jnp.where(allowed, scores, EMPTY)
            top = jnp.maximum(top_ref[...], jnp.max(masked, axis=1, keepdims=True))
            weights = jnp.where(allowed, jnp.exp(masked - top), 0.0)
            factor = jnp.exp(top_ref[...] - top)
            sum_ref[...] = sum_ref[...] * factor + jnp.sum(weights, axis=1, keepdims=True)
            mix_ref[...] = mix_ref[...] * factor + jnp.dot(
                weights.astype(jnp.bfloat16), kv_ref[listed_rows(list_ref, 1, entry), :],
                preferred_element_type=jnp.float32,
            )
            top_ref[...] = top
            return c

        lax.fori_loop(0, info_ref[1 + len(STAGES) + stage, i], step, 0)
    store_mixed(out_ref, mix_ref[...])
    store_stat(stat_ref, 0, sum_ref)
    store_stat(stat_ref, HEADS, top_ref)
    seen = stat_ref[:HEADS, :] > 0.0
    total = jnp.where(seen, stat_ref[:HEADS, :], 1.0)
    stat_ref[HEADS:, :] = jnp.where(seen, stat_ref[HEADS:, :] + jnp.log(total), EMPTY)
    stat_ref[:HEADS, :] = total


def store_mixed(out_ref, mixed):
    for j in range(HEADS):
        out_ref[:, j * HD : (j + 1) * HD] = mixed[j * CH : (j + 1) * CH].astype(out_ref.dtype)


def diagonal(square):
    same = [lax.broadcasted_iota(jnp.int32, (CH, CH), axis) for axis in range(2)]
    return jnp.where(same[0] == same[1], square, 0.0)


def store_stat(stat_ref, start, rows_ref):
    for j in range(HEADS):
        square = rows_ref[j * CH : (j + 1) * CH, :]
        stat_ref[start + j : start + j + 1, :] = jnp.sum(diagonal(square), axis=0, keepdims=True)


def attend_kernel(stage, *refs):
    list_ref, info_ref, q0_ref, q1_ref, qseg_ref, seg_ref = refs[:6]
    refs = refs[6:]
    if stage:
        acc_in_ref, refs = refs[0], refs[1:]
    last = stage == len(STAGES) - 1
    all_pieces = []
    for number in range(0 if last else stage, stage + 1):
        count = max(2, len(STAGES[number])) if number else 1
        all_pieces.append(refs[:count])
        refs = refs[count:]
    if last:
        outs, refs = refs[: 2 * OWN_AND_FAR], refs[2 * OWN_AND_FAR :]
        acc_ref, kv_ref, query_ref, top_ref, sum_ref, mix_ref = refs
    else:
        acc_ref, kv_ref, query_ref = refs
    load_pieces(kv_ref, all_pieces[-1])
    acc_ref[...] = acc_in_ref[...] if stage else jnp.zeros_like(acc_ref)
    for i in range(OWN_AND_FAR):
        load_queries(query_ref, (q0_ref, q1_ref), i)
        plain_pass(i, stage, list_ref, info_ref, query_ref, kv_ref, qseg_ref, seg_ref, acc_ref)
    if not last:
        return
    for i in range(OWN_AND_FAR):
        out_ref, stat_ref = outs[2 * i], outs[2 * i + 1]
        store_stat(stat_ref, 0, acc_ref.at[i, :, HD:])
        total = stat_ref[:HEADS, :]
        fits = (jnp.min(total) >= LEAST) & (jnp.max(total) <= MOST)
        stat_ref[HEADS:, :] = jnp.log(total)
        store_mixed(out_ref, acc_ref[i, :, :HD])

        @pl.when(jnp.logical_not(fits))
        def _(i=i, out_ref=out_ref, stat_ref=stat_ref):
            load_queries(query_ref, (q0_ref, q1_ref), i)
            safe_pass(
                i, list_ref, info_ref, query_ref, all_pieces, kv_ref, qseg_ref, seg_ref,
                out_ref, stat_ref, top_ref, sum_ref, mix_ref,
            )


def attend(stage, listed, info, own_query, far_query, qseg, seg, acc, all_pieces):
    last = stage == len(STAGES) - 1
    pieces = [piece for part in (all_pieces if last else all_pieces[-1:]) for piece in part]
    state = pltpu.VMEM((HEADS * CH, HD), jnp.float32)
    total = (OWN_AND_FAR, HEADS * CH, 2 * HD)
    scratch = [
        pltpu.VMEM((2 * X * 2 * ROWS, HD), jnp.bfloat16),
        pltpu.VMEM((HEADS * CH, HD), jnp.bfloat16),
    ]
    if last:
        shapes = []
        for kind in (jnp.float32, jnp.bfloat16):
            for _ in range(CPD):
                shapes.append(jax.ShapeDtypeStruct((CH, WIDE), kind))
                shapes.append(jax.ShapeDtypeStruct((2 * HEADS, CH), jnp.float32))
        scratch = [pltpu.VMEM(total, jnp.float32)] + scratch + [state] * 3
    else:
        shapes = [jax.ShapeDtypeStruct(total, jnp.float32)]
    begun = [acc] if stage else []
    work = STRETCHES_OF[stage] * CH * OWN_AND_FAR * HEADS * CH
    out = pl.pallas_call(
        functools.partial(attend_kernel, stage),
        out_shape=shapes,
        in_specs=[SMEM, SMEM] + [VMEM] * (4 + len(begun) + len(pieces)),
        out_specs=[VMEM] * len(shapes),
        scratch_shapes=scratch,
        input_output_aliases={6: 0} if stage and not last else {},
        compiler_params=pltpu.CompilerParams(vmem_limit_bytes=VMEM_LIMIT),
        cost_estimate=pl.CostEstimate(
            flops=12 * work * HD, bytes_accessed=4 << 20, transcendentals=work // 2
        ),
        name="attend",
    )(listed, info, own_query, far_query, qseg, seg, *begun, *pieces)
    return out if last else out[0]


def merge_kernel(own_ref, own_stat_ref, got_ref, got_stat_ref, out_ref):
    gap = got_stat_ref[HEADS:, :] - own_stat_ref[HEADS:, :]
    own_share = 1.0 / ((1.0 + jnp.exp(gap)) * own_stat_ref[:HEADS, :])
    got_share = 1.0 / ((1.0 + jnp.exp(-gap)) * got_stat_ref[:HEADS, :])
    for j in range(HEADS):
        own, got = [
            jnp.sum(
                diagonal(jnp.broadcast_to(share[j : j + 1, :], (CH, CH))), axis=1, keepdims=True
            )
            for share in (own_share, got_share)
        ]
        cols = slice(j * HD, (j + 1) * HD)
        out_ref[:, cols] = (
            own_ref[:, cols] * own + got_ref[:, cols].astype(jnp.float32) * got
        ).astype(out_ref.dtype)


def merge(own, own_stat, got, got_stat):
    return pl.pallas_call(
        merge_kernel,
        out_shape=jax.ShapeDtypeStruct(got.shape, jnp.bfloat16),
        in_specs=[VMEM] * 4,
        out_specs=VMEM,
        name="merge",
    )(own, own_stat, got, got_stat)


def project_kernel(wide, index_ref, near0_ref, far0_ref, near1_ref, far1_ref, weight_ref, out_ref):
    lefts = []
    for h in range(NH):
        distance, other = index_ref[0, h], index_ref[1, h]
        both = [
            jnp.where(other == 0, near_ref[distance], far_ref[distance])
            for near_ref, far_ref in ((near0_ref, far0_ref), (near1_ref, far1_ref))
        ]
        lefts.append(jnp.concatenate(both, axis=0))
    for x in range(X):
        total = jnp.zeros((ROWS, 2 * CH), jnp.float32)
        for h in range(NH):
            right = jnp.concatenate([weight_ref[h, e, x] for e in range(2)], axis=1)
            total += jnp.dot(lefts[h], right, preferred_element_type=jnp.float32)
        start = x * 2 * CH
        if wide:
            start = pl.multiple_of(index_ref[2, 0] * (X * 2 * CH) + start, 2 * CH)
        out_ref[:, pl.ds(start, 2 * CH)] = total.astype(out_ref.dtype)


def project(index, gathered, weight, wide):
    feats = weight.shape[3]
    columns = X * 2 * CH
    return pl.pallas_call(
        functools.partial(project_kernel, wide),
        out_shape=jax.ShapeDtypeStruct((ROWS, YL * columns if wide else columns), jnp.bfloat16),
        in_specs=[SMEM] + [VMEM] * 5,
        out_specs=VMEM,
        compiler_params=pltpu.CompilerParams(vmem_limit_bytes=VMEM_LIMIT),
        cost_estimate=pl.CostEstimate(
            flops=2 * ROWS * NH * feats * columns, bytes_accessed=12 << 20, transcendentals=0
        ),
        name="project",
    )(index, *gathered, weight)


def device_number(z, x, yl, h):
    return ((z * X + x) * YL + yl) * NH + h


def weight_moves():
    moves = []
    for z in range(Z):
        for x in range(X):
            for yl in range(YL):
                for h in range(NH):
                    to = device_number(2 * h + yl, x, z % 2, z // 2)
                    moves.append((device_number(z, x, yl, h), to))
    return moves


def fetch(array, axis, by):
    if axis == "y":
        spots = [y % YL * YH + y // YL for y in range(YH * YL)]
        axis = ("ylo", "yhi")
    else:
        spots = list(range({"z": Z, "x": X}[axis]))
    count = len(spots)
    return lax.ppermute(array, axis, [(spots[i], spots[(i - by) % count]) for i in range(count)])


def around(block, axis, count):
    ups, downs = [block], [block]
    for _ in range(count // 2 - 1):
        ups.append(fetch(ups[-1], axis, 1))
        downs.append(fetch(downs[-1], axis, -1))
    half = block.shape[0] // 2
    far = [fetch(ups[-1][:half], axis, 1), fetch(downs[-1][half:], axis, -1)]
    return ups + far + downs[:0:-1]


def gather_x(keys, values):
    block = jnp.concatenate([keys, values], axis=0)
    return [block] + [fetch(block, "x", by) for by in (1, 2, -1)]


def gather_z(blocks):
    rows = around(jnp.concatenate(blocks, axis=0), "z", Z)
    return [(rows[0],)] + [(rows[i], rows[-i]) for i in range(1, Z // 2)] + [tuple(rows[4:6])]


def list_stretches(placement, z, x, ylo):
    item = jnp.arange(LISTED, dtype=jnp.int32)
    per = X * CPD
    order = [dz for stage in STAGES for dz in stage]
    dz = jnp.asarray([order[i // per] for i in range(LISTED)], jnp.int32)
    dx, t = item // CPD % X, item % CPD
    stage = jnp.asarray([n for n, count in enumerate(STRETCHES_OF) for _ in range(count)], jnp.int32)
    start = jnp.asarray([STARTS[n] for n, count in enumerate(STRETCHES_OF) for _ in range(count)], jnp.int32)
    slot = (((z + dz) % Z * X + (x + dx) % X) * YL + ylo) * CPD + t
    pos = placement[slot]
    row = (item - start) // CPD * (2 * CPD) + t
    facts = jnp.stack([row, row + CPD, pos, slot])
    together = stage[None, :] == stage[:, None]
    rank = start + jnp.sum((together & (pos[None, :] < pos[:, None])).astype(jnp.int32), axis=1)
    hit = rank[None, :] == item[:, None]
    return pos, stage, jnp.sum(jnp.where(hit[None], facts[:, None, :], 0), axis=2)


def body(queries, keys, values, out_weight, segment, placement):
    z, x, ylo = lax.axis_index("z"), lax.axis_index("x"), lax.axis_index("ylo")
    yhi, core = lax.axis_index("yhi"), lax.axis_index("core")
    device = (z * X + x) * YL + ylo
    feats = queries.shape[1]

    blocks = gather_x(keys, values)
    far_queries = lax.ppermute(queries, "ylo", SWAP)

    labels = segment.reshape(-1, CH)
    pair_devices = jnp.stack([device, device + 1 - 2 * ylo])
    pair_slots = pair_devices[:, None] * CPD + jnp.arange(CPD, dtype=jnp.int32)[None, :]
    pair_slots = pair_slots.reshape(OWN_AND_FAR)
    pos = placement[pair_slots]
    pair_labels = labels[pair_slots]
    last = pair_labels[:, CH - 1, None]
    beyond = (placement > pos[:, None]) & (labels[:, 0] == last) & (last > 0)
    last_pos = pos + jnp.sum(beyond.astype(jnp.int32), axis=1)
    list_pos, list_stage, listed = list_stretches(placement, z, x, ylo)
    in_stage = list_stage == jnp.arange(len(STAGES), dtype=jnp.int32)[:, None, None]
    full = jnp.sum((in_stage & (list_pos < pos[:, None])).astype(jnp.int32), axis=2)
    some = jnp.sum((in_stage & (list_pos <= last_pos[:, None])).astype(jnp.int32), axis=2)
    info = jnp.concatenate([pos[None], full, some], axis=0)
    qseg = pair_labels.reshape(OWN_AND_FAR * CH, 1)

    moved_weight = lax.ppermute(out_weight, EVERY, weight_moves())
    blocks, listed, info, qseg, moved_weight, far_queries = lax.optimization_barrier(
        (blocks, listed, info, qseg, moved_weight, far_queries)
    )
    weight = lax.all_gather(moved_weight, ("z", "x"), axis=0, tiled=True)
    weight = weight.reshape(NH, 2, X, feats, CH)
    stages = gather_z(blocks)
    state = None
    for stage in range(len(STAGES)):
        state = attend(
            stage, listed, info, queries, far_queries, qseg, labels, state, stages[: stage + 1]
        )
    parts = []
    for t in range(CPD):
        own, own_log, far, far_log = state[2 * t : 2 * t + 2] + state[2 * (CPD + t) : 2 * (CPD + t) + 2]
        parts.append((own, own_log, lax.ppermute(far, "ylo", SWAP), lax.ppermute(far_log, "ylo", SWAP)))
    gathered = []
    for t, part in enumerate(parts):
        near = jnp.concatenate(around(merge(*part), "y", YH * YL), axis=0)
        near = near.reshape(YH * YL, CH, feats)
        if t == CPD - 1:
            near, weight = lax.optimization_barrier((near, weight))
        gathered += [near, lax.ppermute(near, "core", SWAP)]

    def project_group(group, wide):
        h = jnp.arange(NH, dtype=jnp.int32)
        y = h // CORE * YL + group
        distance = (y - (yhi * YL + ylo) + YH * YL) % (YH * YL)
        index = jnp.stack([distance, (h % CORE) ^ core, jnp.broadcast_to(ylo, h.shape)])
        return project(index, gathered, weight, wide)

    theirs = project_group(1 - ylo, False)
    received = lax.ppermute(theirs, "ylo", SWAP)
    mine = project_group(ylo, True)
    return lax.dynamic_update_slice(mine, received, (0, (1 - ylo) * received.shape[1]))


def solution(mesh):
    parts = Mesh(mesh.devices.reshape(Z, X, YL, YH, CORE), EVERY)
    ctx, head = ("z", "x", "ylo"), ("yhi", "core")
    in_specs = (P(ctx, head), P(ctx, head), P(ctx, head), P(head, ctx), P(), P())
    return jax.shard_map(
        body, mesh=parts, in_specs=in_specs, out_specs=P(ctx, head), check_vma=False
    )
```

```python
import functools
import math

import jax
import jax.numpy as jnp
from jax import lax
from jax.experimental import pallas as pl
from jax.experimental.pallas import tpu as pltpu
from jax.sharding import Mesh
from jax.sharding import PartitionSpec as P

HD = 128
CH = 128
CPD = 2
Z, X, YL, YH, CORE = 8, 4, 2, 2, 2
NH = YH * CORE
ZX = Z * X
EVERY = ("z", "x", "ylo", "yhi", "core")
GROUP = 4
HEADS = 8
WIDE = HEADS * HD
LISTED = ZX * CPD
PART = 256
SCALE = 1.0 / math.sqrt(HD)
LEAST = 2.0**-80
MOST = 2.0**100
STAGES = ((0,), (1, 7), (2, 6), (3, 5), (4,))
STRETCHES_OF = [len(stage) * X * CPD for stage in STAGES]
STARTS = [sum(STRETCHES_OF[:i]) for i in range(len(STAGES))]
OWN_AND_FAR = YL * CPD
EMPTY = -1e30
SMEM = pl.BlockSpec(memory_space=pltpu.SMEM)
VMEM = pl.BlockSpec(memory_space=pltpu.VMEM)
NT = (((1,), (1,)), ((), ()))
ROWS = CPD * CH
SWAP = [(0, 1), (1, 0)]
VMEM_LIMIT = 24 << 20


def listed_rows(list_ref, which, entry):
    return pl.ds(pl.multiple_of(list_ref[which, entry] * CH, CH), CH)


def allowed_in(list_ref, seg_ref, entry, q_pos, q_seg):
    k_pos = list_ref[2, entry] * CH + lax.broadcasted_iota(jnp.int32, (CH, CH), 1)
    k_seg = seg_ref[pl.ds(list_ref[3, entry], 1), :]
    return (k_pos <= q_pos) | ((k_seg == q_seg) & (q_seg > 0))


def query_rows(info_ref, qseg_ref, i):
    q_pos = info_ref[0, i] * CH + lax.broadcasted_iota(jnp.int32, (CH, CH), 0)
    q_seg = jnp.broadcast_to(qseg_ref[pl.ds(pl.multiple_of(i * CH, CH), CH), :], (CH, CH))
    return q_pos, q_seg


def load_queries(query_ref, q_refs):
    for i in range(OWN_AND_FAR):
        rows = slice(i % CPD * CH, (i % CPD + 1) * CH)
        for j in range(HEADS):
            query_ref[i, j * CH : (j + 1) * CH, :] = q_refs[i // CPD][rows, j * HD : (j + 1) * HD]


def load_pieces(kv_ref, pieces):
    row = 0
    for piece in pieces:
        rows = piece.shape[0]
        kv_ref[row : row + rows, :] = piece[...]
        row += rows


def plain_pass(i, stage, list_ref, info_ref, q_ref, kv_ref, qseg_ref, seg_ref, acc_ref):
    blocks = HEADS * CH // PART
    base = STARTS[stage]

    def group_step(g, masked):
        entries = [base + g * GROUP + e for e in range(GROUP)]
        key = jnp.concatenate([kv_ref[listed_rows(list_ref, 0, e), :] for e in entries], axis=0)
        value = jnp.concatenate([kv_ref[listed_rows(list_ref, 1, e), :] for e in entries], axis=0)
        value = jnp.concatenate([value, jnp.ones((GROUP * CH, HD), jnp.bfloat16)], axis=1)
        if masked:
            q_pos, q_seg = query_rows(info_ref, qseg_ref, i)
            allowed = jnp.concatenate(
                [allowed_in(list_ref, seg_ref, e, q_pos, q_seg) for e in entries], axis=1
            )
            allowed = jnp.concatenate([allowed] * (PART // CH), axis=0)

        def scores_of(block):
            query = q_ref[i, block * PART : (block + 1) * PART, :]
            return lax.dot_general(query, key, NT, preferred_element_type=jnp.float32)

        ahead = scores_of(0)
        for block in range(blocks):
            scores = ahead
            if block + 1 < blocks:
                ahead = scores_of(block + 1)
            weights = jnp.exp(scores * SCALE)
            if masked:
                weights = jnp.where(allowed, weights, 0.0)
            acc_ref[i, block * PART : (block + 1) * PART, :] += jnp.dot(
                weights.astype(jnp.bfloat16), value, preferred_element_type=jnp.float32
            )

    whole = info_ref[1 + stage, i] // GROUP
    end = (info_ref[1 + len(STAGES) + stage, i] + GROUP - 1) // GROUP
    lax.fori_loop(0, whole, lambda g, c: (group_step(g, False), c)[1], 0)
    lax.fori_loop(whole, end, lambda g, c: (group_step(g, True), c)[1], 0)


def safe_pass(i, list_ref, info_ref, q_ref, kv_ref, qseg_ref, seg_ref, top_ref, sum_ref, mix_ref):
    q_pos, q_seg = query_rows(info_ref, qseg_ref, i)
    top_ref[...] = jnp.full_like(top_ref, EMPTY)
    sum_ref[...] = jnp.zeros_like(sum_ref)
    mix_ref[...] = jnp.zeros_like(mix_ref)

    def step(entry, c):
        @pl.when(list_ref[2, entry] <= info_ref[1 + 2 * len(STAGES), i])
        def _():
            rows = [
                pl.ds(pl.multiple_of((list_ref[which, entry] + list_ref[4, entry]) * CH, CH), CH)
                for which in range(2)
            ]
            allowed = allowed_in(list_ref, seg_ref, entry, q_pos, q_seg)
            allowed = jnp.concatenate([allowed] * HEADS, axis=0)
            scores = SCALE * lax.dot_general(
                q_ref[i], kv_ref[rows[0], :], NT, preferred_element_type=jnp.float32
            )
            masked = jnp.where(allowed, scores, EMPTY)
            top = jnp.maximum(top_ref[...], jnp.max(masked, axis=1, keepdims=True))
            weights = jnp.where(allowed, jnp.exp(masked - top), 0.0)
            factor = jnp.exp(top_ref[...] - top)
            sum_ref[...] = sum_ref[...] * factor + jnp.sum(weights, axis=1, keepdims=True)
            mix_ref[...] = mix_ref[...] * factor + jnp.dot(
                weights.astype(jnp.bfloat16), kv_ref[rows[1], :], preferred_element_type=jnp.float32
            )
            top_ref[...] = top

        return c

    lax.fori_loop(0, LISTED, step, 0)


def store_mixed(out_ref, mixed):
    for j in range(HEADS):
        out_ref[:, j * HD : (j + 1) * HD] = mixed[j * CH : (j + 1) * CH].astype(out_ref.dtype)


def diagonal(square):
    same = [lax.broadcasted_iota(jnp.int32, (CH, CH), axis) for axis in range(2)]
    return jnp.where(same[0] == same[1], square, 0.0)


def store_stat(stat_ref, start, rows_ref):
    for j in range(HEADS):
        square = rows_ref[j * CH : (j + 1) * CH, :]
        stat_ref[start + j : start + j + 1, :] = jnp.sum(diagonal(square), axis=0, keepdims=True)


def attend_kernel(stage, *refs):
    list_ref, info_ref, q0_ref, q1_ref, qseg_ref, seg_ref = refs[:6]
    refs = refs[6:]
    if stage:
        acc_in_ref, refs = refs[0], refs[1:]
    last = stage == len(STAGES) - 1
    all_pieces = []
    for number in range(0 if last else stage, stage + 1):
        count = max(2, len(STAGES[number])) if number else 1
        all_pieces.append(refs[:count])
        refs = refs[count:]
    if last:
        outs, refs = refs[: 2 * OWN_AND_FAR], refs[2 * OWN_AND_FAR :]
        acc_ref, kv_ref, query_ref, top_ref, sum_ref, mix_ref, all_ref, fits_ref = refs
    else:
        acc_ref, kv_ref, query_ref = refs
    load_pieces(kv_ref, all_pieces[-1])
    load_queries(query_ref, (q0_ref, q1_ref))
    acc_ref[...] = acc_in_ref[...] if stage else jnp.zeros_like(acc_ref)

    def stretch(i, c):
        plain_pass(i, stage, list_ref, info_ref, query_ref, kv_ref, qseg_ref, seg_ref, acc_ref)
        return c

    lax.fori_loop(0, OWN_AND_FAR, stretch, 0)
    if not last:
        return
    for i in range(OWN_AND_FAR):
        out_ref, stat_ref = outs[2 * i], outs[2 * i + 1]
        store_stat(stat_ref, 0, acc_ref.at[i, :, HD:])
        total = stat_ref[:HEADS, :]
        fits = (jnp.min(total) >= LEAST) & (jnp.max(total) <= MOST)
        fits_ref[i] = fits.astype(jnp.int32)
        stat_ref[HEADS:, :] = jnp.log(total)
        store_mixed(out_ref, acc_ref[i, :, :HD])

    def again(i, c):
        @pl.when(fits_ref[i] == 0)
        def _():
            load_pieces(all_ref, [piece for pieces in all_pieces for piece in pieces])
            safe_pass(
                i, list_ref, info_ref, query_ref, all_ref, qseg_ref, seg_ref, top_ref, sum_ref, mix_ref
            )
            for number in range(OWN_AND_FAR):

                @pl.when(i == number)
                def _(number=number):
                    out_ref, stat_ref = outs[2 * number], outs[2 * number + 1]
                    store_mixed(out_ref, mix_ref[...])
                    store_stat(stat_ref, 0, sum_ref)
                    store_stat(stat_ref, HEADS, top_ref)
                    seen = stat_ref[:HEADS, :] > 0.0
                    total = jnp.where(seen, stat_ref[:HEADS, :], 1.0)
                    logs = stat_ref[HEADS:, :] + jnp.log(total)
                    stat_ref[HEADS:, :] = jnp.where(seen, logs, EMPTY)
                    stat_ref[:HEADS, :] = total

        return c

    lax.fori_loop(0, OWN_AND_FAR, again, 0)


def attend(stage, listed, info, own_query, far_query, qseg, seg, acc, all_pieces):
    last = stage == len(STAGES) - 1
    pieces = [piece for part in (all_pieces if last else all_pieces[-1:]) for piece in part]
    state = pltpu.VMEM((HEADS * CH, HD), jnp.float32)
    total = (OWN_AND_FAR, HEADS * CH, 2 * HD)
    scratch = [
        pltpu.VMEM((2 * X * 2 * ROWS, HD), jnp.bfloat16),
        pltpu.VMEM((OWN_AND_FAR, HEADS * CH, HD), jnp.bfloat16),
    ]
    if last:
        shapes = []
        for kind in (jnp.float32, jnp.bfloat16):
            for _ in range(CPD):
                shapes.append(jax.ShapeDtypeStruct((CH, WIDE), kind))
                shapes.append(jax.ShapeDtypeStruct((2 * HEADS, CH), jnp.float32))
        scratch = [pltpu.VMEM(total, jnp.float32)] + scratch + [state] * 3
        scratch += [
            pltpu.VMEM((LISTED * 2 * CH, HD), jnp.bfloat16),
            pltpu.SMEM((OWN_AND_FAR,), jnp.int32),
        ]
    else:
        shapes = [jax.ShapeDtypeStruct(total, jnp.float32)]
    begun = [acc] if stage else []
    work = STRETCHES_OF[stage] * CH * OWN_AND_FAR * HEADS * CH
    out = pl.pallas_call(
        functools.partial(attend_kernel, stage),
        out_shape=shapes,
        in_specs=[SMEM, SMEM] + [VMEM] * (4 + len(begun) + len(pieces)),
        out_specs=[VMEM] * len(shapes),
        scratch_shapes=scratch,
        input_output_aliases={6: 0} if stage and not last else {},
        compiler_params=pltpu.CompilerParams(vmem_limit_bytes=VMEM_LIMIT),
        cost_estimate=pl.CostEstimate(
            flops=12 * work * HD, bytes_accessed=4 << 20, transcendentals=work // 2
        ),
        name="attend",
    )(listed, info, own_query, far_query, qseg, seg, *begun, *pieces)
    return out if last else out[0]


def merge_kernel(own_ref, own_stat_ref, got_ref, got_stat_ref, out_ref):
    gap = got_stat_ref[HEADS:, :] - own_stat_ref[HEADS:, :]
    own_share = 1.0 / ((1.0 + jnp.exp(gap)) * own_stat_ref[:HEADS, :])
    got_share = 1.0 / ((1.0 + jnp.exp(-gap)) * got_stat_ref[:HEADS, :])
    for j in range(HEADS):
        own, got = [
            jnp.sum(
                diagonal(jnp.broadcast_to(share[j : j + 1, :], (CH, CH))), axis=1, keepdims=True
            )
            for share in (own_share, got_share)
        ]
        cols = slice(j * HD, (j + 1) * HD)
        out_ref[:, cols] = (
            own_ref[:, cols] * own + got_ref[:, cols].astype(jnp.float32) * got
        ).astype(out_ref.dtype)


def merge(own, own_stat, got, got_stat):
    return pl.pallas_call(
        merge_kernel,
        out_shape=jax.ShapeDtypeStruct(got.shape, jnp.bfloat16),
        in_specs=[VMEM] * 4,
        out_specs=VMEM,
        compiler_params=pltpu.CompilerParams(vmem_limit_bytes=4 << 20),
        cost_estimate=pl.CostEstimate(flops=1 << 20, bytes_accessed=1 << 20, transcendentals=0),
        name="merge",
    )(own, own_stat, got, got_stat)


def project_kernel(wide, index_ref, near0_ref, far0_ref, near1_ref, far1_ref, weight_ref, out_ref):
    lefts = []
    for h in range(NH):
        distance, other = index_ref[0, h], index_ref[1, h]
        both = [
            jnp.where(other == 0, near_ref[distance], far_ref[distance])
            for near_ref, far_ref in ((near0_ref, far0_ref), (near1_ref, far1_ref))
        ]
        lefts.append(jnp.concatenate(both, axis=0))
    for x in range(X):
        total = jnp.zeros((ROWS, 2 * CH), jnp.float32)
        for h in range(NH):
            right = jnp.concatenate([weight_ref[h, e, x] for e in range(2)], axis=1)
            total += jnp.dot(lefts[h], right, preferred_element_type=jnp.float32)
        start = x * 2 * CH
        if wide:
            start = pl.multiple_of(index_ref[2, 0] * (X * 2 * CH) + start, 2 * CH)
        out_ref[:, pl.ds(start, 2 * CH)] = total.astype(out_ref.dtype)


def project(index, gathered, weight, wide):
    feats = weight.shape[3]
    columns = X * 2 * CH
    return pl.pallas_call(
        functools.partial(project_kernel, wide),
        out_shape=jax.ShapeDtypeStruct((ROWS, YL * columns if wide else columns), jnp.bfloat16),
        in_specs=[SMEM] + [VMEM] * 5,
        out_specs=VMEM,
        compiler_params=pltpu.CompilerParams(vmem_limit_bytes=VMEM_LIMIT),
        cost_estimate=pl.CostEstimate(
            flops=2 * ROWS * NH * feats * columns, bytes_accessed=12 << 20, transcendentals=0
        ),
        name="project",
    )(index, *gathered, weight)


def device_number(z, x, yl, h):
    return ((z * X + x) * YL + yl) * NH + h


def weight_moves():
    moves = []
    for z in range(Z):
        for x in range(X):
            for yl in range(YL):
                for h in range(NH):
                    to = device_number(2 * h + yl, x, z % 2, z // 2)
                    moves.append((device_number(z, x, yl, h), to))
    return moves


def fetch(array, axis, by):
    if axis == "y":
        spots = [y % YL * YH + y // YL for y in range(YH * YL)]
        axis = ("ylo", "yhi")
    else:
        spots = list(range({"z": Z, "x": X}[axis]))
    count = len(spots)
    return lax.ppermute(array, axis, [(spots[i], spots[(i - by) % count]) for i in range(count)])


def around(block, axis, count):
    ups, downs = [block], [block]
    for _ in range(count // 2 - 1):
        ups.append(fetch(ups[-1], axis, 1))
        downs.append(fetch(downs[-1], axis, -1))
    half = block.shape[0] // 2
    far = [fetch(ups[-1][:half], axis, 1), fetch(downs[-1][half:], axis, -1)]
    return ups + far + downs[:0:-1]


def gather_x(keys, values):
    block = jnp.concatenate([keys, values], axis=0)
    return [block] + [fetch(block, "x", by) for by in (1, 2, -1)]


def gather_z(blocks):
    rows = around(jnp.concatenate(blocks, axis=0), "z", Z)
    return [(rows[0],)] + [(rows[i], rows[-i]) for i in range(1, Z // 2)] + [tuple(rows[4:6])]


def list_stretches(placement, z, x, ylo):
    item = jnp.arange(LISTED, dtype=jnp.int32)
    per = X * CPD
    order = [dz for stage in STAGES for dz in stage]
    dz = jnp.asarray([order[i // per] for i in range(LISTED)], jnp.int32)
    dx, t = item // CPD % X, item % CPD
    stage = jnp.asarray([n for n, count in enumerate(STRETCHES_OF) for _ in range(count)], jnp.int32)
    start = jnp.asarray([STARTS[n] for n, count in enumerate(STRETCHES_OF) for _ in range(count)], jnp.int32)
    slot = (((z + dz) % Z * X + (x + dx) % X) * YL + ylo) * CPD + t
    pos = placement[slot]
    row = (item - start) // CPD * (2 * CPD) + t
    facts = jnp.stack([row, row + CPD, pos, slot, 2 * start])
    together = stage[None, :] == stage[:, None]
    rank = start + jnp.sum((together & (pos[None, :] < pos[:, None])).astype(jnp.int32), axis=1)
    hit = rank[None, :] == item[:, None]
    return pos, stage, jnp.sum(jnp.where(hit[None], facts[:, None, :], 0), axis=2)


def body(queries, keys, values, out_weight, segment, placement):
    z, x, ylo = lax.axis_index("z"), lax.axis_index("x"), lax.axis_index("ylo")
    yhi, core = lax.axis_index("yhi"), lax.axis_index("core")
    device = (z * X + x) * YL + ylo
    feats = queries.shape[1]

    blocks = gather_x(keys, values)
    far_queries = lax.ppermute(queries, "ylo", SWAP)

    labels = segment.reshape(-1, CH)
    pair_devices = jnp.stack([device, device + 1 - 2 * ylo])
    pair_slots = pair_devices[:, None] * CPD + jnp.arange(CPD, dtype=jnp.int32)[None, :]
    pair_slots = pair_slots.reshape(OWN_AND_FAR)
    pos = placement[pair_slots]
    pair_labels = labels[pair_slots]
    last = pair_labels[:, CH - 1, None]
    beyond = (placement > pos[:, None]) & (labels[:, 0] == last) & (last > 0)
    last_pos = pos + jnp.sum(beyond.astype(jnp.int32), axis=1)
    list_pos, list_stage, listed = list_stretches(placement, z, x, ylo)
    in_stage = list_stage == jnp.arange(len(STAGES), dtype=jnp.int32)[:, None, None]
    full = jnp.sum((in_stage & (list_pos < pos[:, None])).astype(jnp.int32), axis=2)
    some = jnp.sum((in_stage & (list_pos <= last_pos[:, None])).astype(jnp.int32), axis=2)
    info = jnp.concatenate([pos[None], full, some, last_pos[None]], axis=0)
    qseg = pair_labels.reshape(OWN_AND_FAR * CH, 1)

    moved_weight = lax.ppermute(out_weight, EVERY, weight_moves())
    blocks, listed, info, qseg, moved_weight, far_queries = lax.optimization_barrier(
        (blocks, listed, info, qseg, moved_weight, far_queries)
    )
    weight = lax.all_gather(moved_weight, ("z", "x"), axis=0, tiled=True)
    weight = weight.reshape(NH, 2, X, feats, CH)
    stages = gather_z(blocks)
    state = None
    for stage in range(len(STAGES)):
        state = attend(
            stage, listed, info, queries, far_queries, qseg, labels, state, stages[: stage + 1]
        )
    parts = []
    for t in range(CPD):
        own, own_log, far, far_log = state[2 * t : 2 * t + 2] + state[2 * (CPD + t) : 2 * (CPD + t) + 2]
        parts.append((own, own_log, lax.ppermute(far, "ylo", SWAP), lax.ppermute(far_log, "ylo", SWAP)))
    gathered = []
    for t, part in enumerate(parts):
        near = jnp.concatenate(around(merge(*part), "y", YH * YL), axis=0)
        near = near.reshape(YH * YL, CH, feats)
        if t == CPD - 1:
            near, weight = lax.optimization_barrier((near, weight))
        gathered += [near, lax.ppermute(near, "core", SWAP)]

    def project_group(group, wide):
        h = jnp.arange(NH, dtype=jnp.int32)
        y = h // CORE * YL + group
        distance = (y - (yhi * YL + ylo) + YH * YL) % (YH * YL)
        index = jnp.stack([distance, (h % CORE) ^ core, jnp.broadcast_to(ylo, h.shape)])
        return project(index, gathered, weight, wide)

    theirs = project_group(1 - ylo, False)
    received = lax.ppermute(theirs, "ylo", SWAP)
    mine = project_group(ylo, True)
    return lax.dynamic_update_slice(mine, received, (0, (1 - ylo) * received.shape[1]))


def solution(mesh):
    parts = Mesh(mesh.devices.reshape(Z, X, YL, YH, CORE), EVERY)
    ctx, head = ("z", "x", "ylo"), ("yhi", "core")
    in_specs = (P(ctx, head), P(ctx, head), P(ctx, head), P(head, ctx), P(), P())
    return jax.shard_map(
        body, mesh=parts, in_specs=in_specs, out_specs=P(ctx, head), check_vma=False
    )
```

```python
import functools
import math

import jax
import jax.numpy as jnp
from jax import lax
from jax.experimental import pallas as pl
from jax.experimental.pallas import tpu as pltpu
from jax.sharding import Mesh
from jax.sharding import PartitionSpec as P

HD = 128
CH = 128
CPD = 2
Z, X, YL, YH, CORE = 8, 4, 2, 2, 2
NH = YH * CORE
ZX = Z * X
EVERY = ("z", "x", "ylo", "yhi", "core")
GROUP = 4
HEADS = 8
WIDE = HEADS * HD
LISTED = ZX * CPD
PART = 256
SCALE = 1.0 / math.sqrt(HD)
LEAST = 2.0**-80
MOST = 2.0**100
STAGES = ((0,), (1, 7), (2, 6), (3, 5), (4,))
STRETCHES_OF = [len(stage) * X * CPD for stage in STAGES]
STARTS = [sum(STRETCHES_OF[:i]) for i in range(len(STAGES))]
OWN_AND_FAR = YL * CPD
EMPTY = -1e30
SMEM = pl.BlockSpec(memory_space=pltpu.SMEM)
VMEM = pl.BlockSpec(memory_space=pltpu.VMEM)
NT = (((1,), (1,)), ((), ()))
ROWS = CPD * CH
SWAP = [(0, 1), (1, 0)]
VMEM_LIMIT = 24 << 20


def listed_rows(list_ref, which, entry):
    return pl.ds(pl.multiple_of(list_ref[which, entry] * CH, CH), CH)


def allowed_in(list_ref, seg_ref, entry, q_pos, q_seg):
    k_pos = list_ref[2, entry] * CH + lax.broadcasted_iota(jnp.int32, (CH, CH), 1)
    k_seg = seg_ref[pl.ds(list_ref[3, entry], 1), :]
    return (k_pos <= q_pos) | ((k_seg == q_seg) & (q_seg > 0))


def query_rows(info_ref, qseg_ref, i):
    q_pos = info_ref[0, i] * CH + lax.broadcasted_iota(jnp.int32, (CH, CH), 0)
    q_seg = jnp.broadcast_to(qseg_ref[pl.ds(pl.multiple_of(i * CH, CH), CH), :], (CH, CH))
    return q_pos, q_seg


def load_queries(query_ref, q_refs):
    for i in range(OWN_AND_FAR):
        rows = slice(i % CPD * CH, (i % CPD + 1) * CH)
        for j in range(HEADS):
            query_ref[i, j * CH : (j + 1) * CH, :] = q_refs[i // CPD][rows, j * HD : (j + 1) * HD]


def load_pieces(kv_ref, pieces):
    row = 0
    for piece in pieces:
        rows = piece.shape[0]
        kv_ref[row : row + rows, :] = piece[...]
        row += rows


def plain_pass(i, stage, list_ref, info_ref, q_ref, kv_ref, qseg_ref, seg_ref, acc_ref):
    blocks = HEADS * CH // PART
    base = STARTS[stage]

    def group_step(g, masked):
        entries = [base + g * GROUP + e for e in range(GROUP)]
        key = jnp.concatenate([kv_ref[listed_rows(list_ref, 0, e), :] for e in entries], axis=0)
        value = jnp.concatenate([kv_ref[listed_rows(list_ref, 1, e), :] for e in entries], axis=0)
        value = jnp.concatenate([value, jnp.ones((GROUP * CH, HD), jnp.bfloat16)], axis=1)
        if masked:
            q_pos, q_seg = query_rows(info_ref, qseg_ref, i)
            allowed = jnp.concatenate(
                [allowed_in(list_ref, seg_ref, e, q_pos, q_seg) for e in entries], axis=1
            )
            allowed = jnp.concatenate([allowed] * (PART // CH), axis=0)

        def scores_of(block):
            query = q_ref[i, block * PART : (block + 1) * PART, :]
            return lax.dot_general(query, key, NT, preferred_element_type=jnp.float32)

        ahead = scores_of(0)
        for block in range(blocks):
            scores = ahead
            if block + 1 < blocks:
                ahead = scores_of(block + 1)
            weights = jnp.exp(scores * SCALE)
            if masked:
                weights = jnp.where(allowed, weights, 0.0)
            acc_ref[i, block * PART : (block + 1) * PART, :] += jnp.dot(
                weights.astype(jnp.bfloat16), value, preferred_element_type=jnp.float32
            )

    whole = info_ref[1 + stage, i] // GROUP
    end = (info_ref[1 + len(STAGES) + stage, i] + GROUP - 1) // GROUP
    lax.fori_loop(0, whole, lambda g, c: (group_step(g, False), c)[1], 0)
    lax.fori_loop(whole, end, lambda g, c: (group_step(g, True), c)[1], 0)


def safe_pass(i, list_ref, info_ref, q_ref, kv_ref, qseg_ref, seg_ref, top_ref, sum_ref, mix_ref):
    q_pos, q_seg = query_rows(info_ref, qseg_ref, i)
    top_ref[...] = jnp.full_like(top_ref, EMPTY)
    sum_ref[...] = jnp.zeros_like(sum_ref)
    mix_ref[...] = jnp.zeros_like(mix_ref)

    def step(entry, c):
        @pl.when(list_ref[2, entry] <= info_ref[1 + 2 * len(STAGES), i])
        def _():
            rows = [
                pl.ds(pl.multiple_of((list_ref[which, entry] + list_ref[4, entry]) * CH, CH), CH)
                for which in range(2)
            ]
            allowed = allowed_in(list_ref, seg_ref, entry, q_pos, q_seg)
            allowed = jnp.concatenate([allowed] * HEADS, axis=0)
            scores = SCALE * lax.dot_general(
                q_ref[i], kv_ref[rows[0], :], NT, preferred_element_type=jnp.float32
            )
            masked = jnp.where(allowed, scores, EMPTY)
            top = jnp.maximum(top_ref[...], jnp.max(masked, axis=1, keepdims=True))
            weights = jnp.where(allowed, jnp.exp(masked - top), 0.0)
            factor = jnp.exp(top_ref[...] - top)
            sum_ref[...] = sum_ref[...] * factor + jnp.sum(weights, axis=1, keepdims=True)
            mix_ref[...] = mix_ref[...] * factor + jnp.dot(
                weights.astype(jnp.bfloat16), kv_ref[rows[1], :], preferred_element_type=jnp.float32
            )
            top_ref[...] = top

        return c

    lax.fori_loop(0, LISTED, step, 0)


def store_mixed(out_ref, mixed):
    for j in range(HEADS):
        out_ref[:, j * HD : (j + 1) * HD] = mixed[j * CH : (j + 1) * CH].astype(out_ref.dtype)


def diagonal(square):
    same = [lax.broadcasted_iota(jnp.int32, (CH, CH), axis) for axis in range(2)]
    return jnp.where(same[0] == same[1], square, 0.0)


def store_stat(stat_ref, start, rows_ref):
    for j in range(HEADS):
        square = rows_ref[j * CH : (j + 1) * CH, :]
        stat_ref[start + j : start + j + 1, :] = jnp.sum(diagonal(square), axis=0, keepdims=True)


def attend_kernel(stage, *refs):
    list_ref, info_ref, q0_ref, q1_ref, qseg_ref, seg_ref = refs[:6]
    refs = refs[6:]
    if stage:
        acc_in_ref, refs = refs[0], refs[1:]
    last = stage == len(STAGES) - 1
    all_pieces = []
    for number in range(0 if last else stage, stage + 1):
        count = max(2, len(STAGES[number])) if number else 1
        all_pieces.append(refs[:count])
        refs = refs[count:]
    if last:
        outs, refs = refs[: 3 * CPD + 1], refs[3 * CPD + 1 :]
        acc_ref, kv_ref, query_ref, top_ref, sum_ref, mix_ref, all_ref, fits_ref = refs
    else:
        acc_ref, kv_ref, query_ref = refs
    load_pieces(kv_ref, all_pieces[-1])
    load_queries(query_ref, (q0_ref, q1_ref))
    acc_ref[...] = acc_in_ref[...] if stage else jnp.zeros_like(acc_ref)

    def stretch(i, c):
        plain_pass(i, stage, list_ref, info_ref, query_ref, kv_ref, qseg_ref, seg_ref, acc_ref)
        return c

    lax.fori_loop(0, OWN_AND_FAR, stretch, 0)
    if not last:
        return

    def results(i):
        if i < CPD:
            return outs[2 * i], outs[2 * i + 1]
        return outs[CPD + i], outs[3 * CPD].at[i - CPD]

    for i in range(OWN_AND_FAR):
        out_ref, stat_ref = results(i)
        store_stat(stat_ref, 0, acc_ref.at[i, :, HD:])
        total = stat_ref[:HEADS, :]
        fits = (jnp.min(total) >= LEAST) & (jnp.max(total) <= MOST)
        fits_ref[i] = fits.astype(jnp.int32)
        stat_ref[HEADS:, :] = jnp.log(total)
        store_mixed(out_ref, acc_ref[i, :, :HD])

    def again(i, c):
        @pl.when(fits_ref[i] == 0)
        def _():
            load_pieces(all_ref, [piece for pieces in all_pieces for piece in pieces])
            safe_pass(
                i, list_ref, info_ref, query_ref, all_ref, qseg_ref, seg_ref, top_ref, sum_ref, mix_ref
            )
            for number in range(OWN_AND_FAR):

                @pl.when(i == number)
                def _(number=number):
                    out_ref, stat_ref = results(number)
                    store_mixed(out_ref, mix_ref[...])
                    store_stat(stat_ref, 0, sum_ref)
                    store_stat(stat_ref, HEADS, top_ref)
                    seen = stat_ref[:HEADS, :] > 0.0
                    total = jnp.where(seen, stat_ref[:HEADS, :], 1.0)
                    logs = stat_ref[HEADS:, :] + jnp.log(total)
                    stat_ref[HEADS:, :] = jnp.where(seen, logs, EMPTY)
                    stat_ref[:HEADS, :] = total

        return c

    lax.fori_loop(0, OWN_AND_FAR, again, 0)


def attend(stage, listed, info, own_query, far_query, qseg, seg, acc, all_pieces):
    last = stage == len(STAGES) - 1
    pieces = [piece for part in (all_pieces if last else all_pieces[-1:]) for piece in part]
    state = pltpu.VMEM((HEADS * CH, HD), jnp.float32)
    total = (OWN_AND_FAR, HEADS * CH, 2 * HD)
    scratch = [
        pltpu.VMEM((2 * X * 2 * ROWS, HD), jnp.bfloat16),
        pltpu.VMEM((OWN_AND_FAR, HEADS * CH, HD), jnp.bfloat16),
    ]
    if last:
        shapes = []
        for _ in range(CPD):
            shapes.append(jax.ShapeDtypeStruct((CH, WIDE), jnp.float32))
            shapes.append(jax.ShapeDtypeStruct((2 * HEADS, CH), jnp.float32))
        shapes += [jax.ShapeDtypeStruct((CH, WIDE), jnp.bfloat16)] * CPD
        shapes.append(jax.ShapeDtypeStruct((CPD, 2 * HEADS, CH), jnp.float32))
        scratch = [pltpu.VMEM(total, jnp.float32)] + scratch + [state] * 3
        scratch += [
            pltpu.VMEM((LISTED * 2 * CH, HD), jnp.bfloat16),
            pltpu.SMEM((OWN_AND_FAR,), jnp.int32),
        ]
    else:
        shapes = [jax.ShapeDtypeStruct(total, jnp.float32)]
    begun = [acc] if stage else []
    work = STRETCHES_OF[stage] * CH * OWN_AND_FAR * HEADS * CH
    out = pl.pallas_call(
        functools.partial(attend_kernel, stage),
        out_shape=shapes,
        in_specs=[SMEM, SMEM] + [VMEM] * (4 + len(begun) + len(pieces)),
        out_specs=[VMEM] * len(shapes),
        scratch_shapes=scratch,
        input_output_aliases={6: 0} if stage and not last else {},
        compiler_params=pltpu.CompilerParams(vmem_limit_bytes=VMEM_LIMIT),
        cost_estimate=pl.CostEstimate(
            flops=12 * work * HD, bytes_accessed=4 << 20, transcendentals=work // 2
        ),
        name="attend",
    )(listed, info, own_query, far_query, qseg, seg, *begun, *pieces)
    return out if last else out[0]


def merge_kernel(t, own_ref, own_stat_ref, got_ref, got_stats_ref, out_ref):
    got_stat_ref = got_stats_ref.at[t]
    gap = got_stat_ref[HEADS:, :] - own_stat_ref[HEADS:, :]
    own_share = 1.0 / ((1.0 + jnp.exp(gap)) * own_stat_ref[:HEADS, :])
    got_share = 1.0 / ((1.0 + jnp.exp(-gap)) * got_stat_ref[:HEADS, :])
    for j in range(HEADS):
        own, got = [
            jnp.sum(
                diagonal(jnp.broadcast_to(share[j : j + 1, :], (CH, CH))), axis=1, keepdims=True
            )
            for share in (own_share, got_share)
        ]
        cols = slice(j * HD, (j + 1) * HD)
        out_ref[:, cols] = (
            own_ref[:, cols] * own + got_ref[:, cols].astype(jnp.float32) * got
        ).astype(out_ref.dtype)


def merge(t, own, own_stat, got, got_stats):
    return pl.pallas_call(
        functools.partial(merge_kernel, t),
        out_shape=jax.ShapeDtypeStruct(got.shape, jnp.bfloat16),
        in_specs=[VMEM] * 4,
        out_specs=VMEM,
        compiler_params=pltpu.CompilerParams(vmem_limit_bytes=4 << 20),
        cost_estimate=pl.CostEstimate(flops=1 << 20, bytes_accessed=1 << 20, transcendentals=0),
        name="merge",
    )(own, own_stat, got, got_stats)


def project_kernel(wide, index_ref, near0_ref, far0_ref, near1_ref, far1_ref, weight_ref, out_ref):
    lefts = []
    for h in range(NH):
        distance, other = index_ref[0, h], index_ref[1, h]
        both = [
            jnp.where(other == 0, near_ref[distance], far_ref[distance])
            for near_ref, far_ref in ((near0_ref, far0_ref), (near1_ref, far1_ref))
        ]
        lefts.append(jnp.concatenate(both, axis=0))
    for x in range(X):
        total = jnp.zeros((ROWS, 2 * CH), jnp.float32)
        for h in range(NH):
            right = jnp.concatenate([weight_ref[h, e, x] for e in range(2)], axis=1)
            total += jnp.dot(lefts[h], right, preferred_element_type=jnp.float32)
        start = x * 2 * CH
        if wide:
            start = pl.multiple_of(index_ref[2, 0] * (X * 2 * CH) + start, 2 * CH)
        out_ref[:, pl.ds(start, 2 * CH)] = total.astype(out_ref.dtype)


def project(index, gathered, weight, wide):
    feats = weight.shape[3]
    columns = X * 2 * CH
    return pl.pallas_call(
        functools.partial(project_kernel, wide),
        out_shape=jax.ShapeDtypeStruct((ROWS, YL * columns if wide else columns), jnp.bfloat16),
        in_specs=[SMEM] + [VMEM] * 5,
        out_specs=VMEM,
        compiler_params=pltpu.CompilerParams(vmem_limit_bytes=VMEM_LIMIT),
        cost_estimate=pl.CostEstimate(
            flops=2 * ROWS * NH * feats * columns, bytes_accessed=12 << 20, transcendentals=0
        ),
        name="project",
    )(index, *gathered, weight)


def device_number(z, x, yl, h):
    return ((z * X + x) * YL + yl) * NH + h


def weight_moves():
    moves = []
    for z in range(Z):
        for x in range(X):
            for yl in range(YL):
                for h in range(NH):
                    to = device_number(2 * h + yl, x, z % 2, z // 2)
                    moves.append((device_number(z, x, yl, h), to))
    return moves


def fetch(array, axis, by):
    if axis == "y":
        spots = [y % YL * YH + y // YL for y in range(YH * YL)]
        axis = ("ylo", "yhi")
    else:
        spots = list(range({"z": Z, "x": X}[axis]))
    count = len(spots)
    return lax.ppermute(array, axis, [(spots[i], spots[(i - by) % count]) for i in range(count)])


def around(block, axis, count):
    ups, downs = [block], [block]
    for _ in range(count // 2 - 1):
        ups.append(fetch(ups[-1], axis, 1))
        downs.append(fetch(downs[-1], axis, -1))
    half = block.shape[0] // 2
    far = [fetch(ups[-1][:half], axis, 1), fetch(downs[-1][half:], axis, -1)]
    return ups + far + downs[:0:-1]


def gather_x(keys, values):
    block = jnp.concatenate([keys, values], axis=0)
    return [block] + [fetch(block, "x", by) for by in (1, 2, -1)]


def gather_z(blocks):
    rows = around(jnp.concatenate(blocks, axis=0), "z", Z)
    return [(rows[0],)] + [(rows[i], rows[-i]) for i in range(1, Z // 2)] + [tuple(rows[4:6])]


def list_stretches(placement, z, x, ylo):
    item = jnp.arange(LISTED, dtype=jnp.int32)
    per = X * CPD
    order = [dz for stage in STAGES for dz in stage]
    dz = jnp.asarray([order[i // per] for i in range(LISTED)], jnp.int32)
    dx, t = item // CPD % X, item % CPD
    stage = jnp.asarray([n for n, count in enumerate(STRETCHES_OF) for _ in range(count)], jnp.int32)
    start = jnp.asarray([STARTS[n] for n, count in enumerate(STRETCHES_OF) for _ in range(count)], jnp.int32)
    slot = (((z + dz) % Z * X + (x + dx) % X) * YL + ylo) * CPD + t
    slots = jnp.arange(ZX * YL * CPD, dtype=jnp.int32)
    pos = jnp.sum(jnp.where(slot[:, None] == slots, placement[None, :], 0), axis=1)
    row = (item - start) // CPD * (2 * CPD) + t
    facts = jnp.stack([row, row + CPD, pos, slot, 2 * start])
    together = stage[None, :] == stage[:, None]
    rank = start + jnp.sum((together & (pos[None, :] < pos[:, None])).astype(jnp.int32), axis=1)
    hit = rank[None, :] == item[:, None]
    return pos, stage, jnp.sum(jnp.where(hit[None], facts[:, None, :], 0), axis=2)


def body(queries, keys, values, out_weight, segment, placement):
    z, x, ylo = lax.axis_index("z"), lax.axis_index("x"), lax.axis_index("ylo")
    yhi, core = lax.axis_index("yhi"), lax.axis_index("core")
    feats = queries.shape[1]

    blocks = gather_x(keys, values)
    far_queries = lax.ppermute(queries, "ylo", SWAP)

    labels = segment.reshape(-1, CH)
    first_slot = (z * X + x) * OWN_AND_FAR
    turn = jnp.arange(OWN_AND_FAR, dtype=jnp.int32) ^ (ylo * CPD)
    turned = turn[:, None] == jnp.arange(OWN_AND_FAR, dtype=jnp.int32)
    pair_pos = lax.dynamic_slice_in_dim(placement, first_slot, OWN_AND_FAR, 0)
    pos = jnp.sum(jnp.where(turned, pair_pos[None, :], 0), axis=1)
    pair_labels = lax.dynamic_slice_in_dim(labels, first_slot, OWN_AND_FAR, 0)
    pair_labels = jnp.where(
        ylo == 0, pair_labels, jnp.concatenate([pair_labels[CPD:], pair_labels[:CPD]], axis=0)
    )
    last = pair_labels[:, CH - 1, None]
    beyond = (placement > pos[:, None]) & (labels[:, 0] == last) & (last > 0)
    last_pos = pos + jnp.sum(beyond.astype(jnp.int32), axis=1)
    list_pos, list_stage, listed = list_stretches(placement, z, x, ylo)
    in_stage = list_stage == jnp.arange(len(STAGES), dtype=jnp.int32)[:, None, None]
    full = jnp.sum((in_stage & (list_pos < pos[:, None])).astype(jnp.int32), axis=2)
    some = jnp.sum((in_stage & (list_pos <= last_pos[:, None])).astype(jnp.int32), axis=2)
    info = jnp.concatenate([pos[None], full, some, last_pos[None]], axis=0)
    qseg = pair_labels.reshape(OWN_AND_FAR * CH, 1)

    moved_weight = lax.ppermute(out_weight, EVERY, weight_moves())
    blocks, listed, info, qseg, moved_weight, far_queries = lax.optimization_barrier(
        (blocks, listed, info, qseg, moved_weight, far_queries)
    )
    weight = lax.all_gather(moved_weight, ("z", "x"), axis=0, tiled=True)
    weight = weight.reshape(NH, 2, X, feats, CH)
    stages = gather_z(blocks)
    state = None
    for stage in range(len(STAGES)):
        state = attend(
            stage, listed, info, queries, far_queries, qseg, labels, state, stages[: stage + 1]
        )
    got_stats = lax.ppermute(state[3 * CPD], "ylo", SWAP)
    parts = [
        (t, state[2 * t], state[2 * t + 1], lax.ppermute(state[2 * CPD + t], "ylo", SWAP), got_stats)
        for t in range(CPD)
    ]
    gathered = []
    for part in parts:
        near = jnp.concatenate(around(merge(*part), "y", YH * YL), axis=0)
        near = near.reshape(YH * YL, CH, feats)
        if part[0] == CPD - 1:
            near, weight = lax.optimization_barrier((near, weight))
        gathered += [near, lax.ppermute(near, "core", SWAP)]

    def project_group(group, wide):
        h = jnp.arange(NH, dtype=jnp.int32)
        y = h // CORE * YL + group
        distance = (y - (yhi * YL + ylo) + YH * YL) % (YH * YL)
        index = jnp.stack([distance, (h % CORE) ^ core, jnp.broadcast_to(ylo, h.shape)])
        return project(index, gathered, weight, wide)

    theirs = project_group(1 - ylo, False)
    received = lax.ppermute(theirs, "ylo", SWAP)
    mine = project_group(ylo, True)
    return lax.dynamic_update_slice(mine, received, (0, (1 - ylo) * received.shape[1]))


def solution(mesh):
    parts = Mesh(mesh.devices.reshape(Z, X, YL, YH, CORE), EVERY)
    ctx, head = ("z", "x", "ylo"), ("yhi", "core")
    in_specs = (P(ctx, head), P(ctx, head), P(ctx, head), P(head, ctx), P(), P())
    return jax.shard_map(
        body, mesh=parts, in_specs=in_specs, out_specs=P(ctx, head), check_vma=False
    )
```
